128 devices in a mesh: dp: 16 (over y, z), tensor: 8 (over x, core).
Axes of the slice: x: 4, y: 4, z: 4, core: 2. Of those that a mesh axis runs over, the one named last changes fastest.
Arguments:
- activations: bfloat16 [16384, 6144], P(('dp', 'tensor')), may hold values from -6 to 6
- cotangent: bfloat16 [16384, 3072], P('dp', 'tensor'), may hold values from -6 to 6
- weight: bfloat16 [6144, 3072], P(None, 'tensor'), may hold values from -0.109375 to 0.109375
- residual: bfloat16 [16, 6144, 3072], P('dp', None, 'tensor'), may hold values from -4 to 4
- warm_factor: float32 [3072, 32], P('tensor'), may hold values from -6 to 6
Outputs:
- new_factor: float32 [3072, 32], P('tensor')
- new_residual: bfloat16 [16, 6144, 3072], P('dp', None, 'tensor')
- input_grads: bfloat16 [16384, 6144], P(('dp', 'tensor'))
The draws below stay inside these ranges and needn't reach their ends.
All inputs are finite; a program needn't handle non-finite values.
Results may differ from the reference program's by a relative error of at most 0.001.
Values may be sent and summed in bfloat16 or wider, within the bound.
No kernel may reach another device: no remote copies, remote signals or barrier semaphores. Data moves between devices by JAX's collectives and lax.ppermute only.
A program may use at most 128 MiB of HBM per device.

```python
import jax
import jax.numpy as jnp
from jax import lax

D = 6144
HEAD_DIM = 128
HEADS = 24
RANK = 32
TOK_DEV = 1024
TOKENS = 16384
COLS = 3072
N_DP = 16


def block_levels(stream_key, extent, split, smallest, largest):
    def one(axis_at, shards_of):
        heights = jax.random.uniform(jax.random.fold_in(jax.random.fold_in(stream_key, 6), axis_at), (shards_of,), jnp.float32, smallest / len(split), largest / len(split))
        return jnp.repeat(jnp.exp(heights), extent[axis_at] // shards_of).reshape((-1,) + (1,) * (len(extent) - axis_at - 1))

    gain = one(*split[0])
    for cut in split[1:]:
        gain = gain * one(*cut)
    return gain


def bell_draw(rng, shape, width, bound, split=(), kind=jnp.bfloat16):
    gain = block_levels(rng, shape, split, -0.22, 0.18) if split else 1.0
    drawn = jax.random.normal(rng, shape, jnp.float32) * width * gain
    return jnp.minimum(jnp.maximum(drawn, -bound), bound).astype(kind)


def setup_inputs(seed: int = 0) -> dict:
    seeds = jax.random.split(jax.random.key(seed), 6)
    return {
        "activations": bell_draw(seeds[0], (TOKENS, D), 1.0, 6.0, ((0, 128),)),
        "cotangent": bell_draw(seeds[1], (TOKENS, COLS), 1.0, 6.0, ((0, 16), (1, 8))),
        "weight": bell_draw(seeds[2], (D, COLS), COLS ** -0.5, 0.109375, ((1, 8),)),
        "residual": bell_draw(seeds[3], (N_DP, D, COLS), 0.5, 4.0, ((0, 16), (2, 8))),
        "warm_factor": bell_draw(seeds[4], (COLS, RANK), 1.0, 6.0, ((0, 8),), jnp.float32),
    }


def orthonormal(matrix):
    gram_small = jnp.dot(matrix.T, matrix, precision=lax.Precision.HIGHEST)
    factor_low = jnp.linalg.cholesky(gram_small)
    return lax.linalg.triangular_solve(factor_low, matrix, left_side=False, lower=True, transpose_a=True)

def reference(activations, cotangent, weight, residual, warm_factor):
    token_scale = TOK_DEV ** (-0.5)
    act_groups = activations.reshape(N_DP, TOK_DEV, D)
    cot_groups = cotangent.reshape(N_DP, TOK_DEV, HEADS * HEAD_DIM)

    def merge_one(member):
        gradient = jnp.dot(act_groups[member].T.astype(jnp.float32), cot_groups[member].astype(jnp.float32), preferred_element_type=jnp.float32)
        return gradient * token_scale + residual[member].astype(jnp.float32)
    members = jnp.arange(N_DP, dtype=jnp.int32)
    merged = lax.map(merge_one, members)
    left_terms = lax.map(lambda member: jnp.dot(merged[member], warm_factor, precision=lax.Precision.HIGHEST), members)
    left = jnp.sum(left_terms, axis=0)
    basis_full = orthonormal(left)
    right_terms = lax.map(lambda member: jnp.dot(merged[member].T, basis_full, precision=lax.Precision.HIGHEST), members)
    new_factor = jnp.sum(right_terms, axis=0) / N_DP
    approx = jnp.dot(basis_full, new_factor.T, precision=lax.Precision.HIGHEST)
    new_residual = lax.map(lambda member: (merged[member] - approx).astype(jnp.bfloat16), members)
    input_grads = lax.dot_general(cotangent.astype(jnp.float32), weight.astype(jnp.float32), (((1,), (1,)), ((), ())), preferred_element_type=jnp.float32).astype(jnp.bfloat16)
    return (new_factor, new_residual, input_grads)
```

```python
import functools

import jax
import jax.numpy as jnp
from jax import lax
from jax.experimental import pallas as pl
from jax.experimental.pallas import tpu as pltpu
from jax.sharding import Mesh, PartitionSpec as P

BF16, F32 = jnp.bfloat16, jnp.float32
SIZE = {"y": 4, "z": 4, "x": 4, "core": 2}
VMEM_LIMIT = 56 * 1024 * 1024


def shift(value, axis, step):
    n = SIZE[axis]
    return lax.ppermute(value, axis, [(i, (i + step) % n) for i in range(n)])


def split3(value):
    high = lax.reduce_precision(value, 8, 7)
    rest = value - high
    mid = lax.reduce_precision(rest, 8, 7)
    return high.astype(BF16), mid.astype(BF16), (rest - mid).astype(BF16)


def fold3(value):
    rows = value.shape[0] // 3
    return value[:rows] + value[rows : 2 * rows] + value[2 * rows :]


def mm(a, b, ca, cb):
    return lax.dot_general(a, b, (((ca,), (cb,)), ((), ())), preferred_element_type=F32)


def block(value, index):
    return lax.dynamic_index_in_dim(value, index, 0, False)


def reduce_scatter(value, axis):
    n, me = SIZE[axis], lax.axis_index(axis)
    parts = [shift(block(value, (me + s) % n), axis, s) for s in range(1, n)]
    total = block(value, me)
    for part in parts:
        total = total + part
    return total


def all_sum(value, axis):
    parts = [shift(value, axis, s) for s in range(1, SIZE[axis])]
    for part in parts:
        value = value + part
    return value


def all_blocks(value, axis):
    n, me = SIZE[axis], lax.axis_index(axis)
    parts = [value] + [shift(value, axis, s) for s in range(1, n)]
    result = jnp.zeros((n,) + value.shape, value.dtype)
    for s, part in enumerate(parts):
        result = lax.dynamic_update_index_in_dim(result, part, (me - s) % n, 0)
    return result


def ring(value, axis, halves):
    low = shift(value, axis, 1)
    high = shift(value, axis, -1)
    first, second = halves
    far_a = shift(first(low), axis, 1)
    far_b = shift(second(high), axis, -1)
    return low, high, far_a, far_b


def inverse_kernel(gram_ref, out_ref):
    n = gram_ref.shape[0]
    row = lax.broadcasted_iota(jnp.int32, (n, 2 * n), 0)
    col = lax.broadcasted_iota(jnp.int32, (n, 2 * n), 1)
    eye = jnp.where(row + n == col, 1.0, 0.0).astype(F32)
    work = jnp.concatenate([gram_ref[...], jnp.zeros((n, n), F32)], axis=1) + eye
    for k in range(n):
        pivot_row = work[k : k + 1, :]
        pivot = jnp.sum(jnp.where(col[:1] == k, pivot_row, 0.0), axis=1, keepdims=True)
        column = jnp.sum(jnp.where(col == k, work, 0.0), axis=1, keepdims=True)
        factor = jnp.where(row[:, :1] > k, column / pivot, 0.0)
        root = lax.rsqrt(pivot)
        root = root * (1.5 - 0.5 * pivot * root * root)
        scale = jnp.where(row[:, :1] == k, root, 1.0)
        work = (work - factor * pivot_row) * scale
    out_ref[...] = work[:, n:]


def inverse_of_factor(gram):
    return pl.pallas_call(
        inverse_kernel,
        out_shape=jax.ShapeDtypeStruct(gram.shape, F32),
        name="inverse_of_factor",
    )(gram)


def grad_kernel(groups, final, starts_ref, *refs):
    n = sum(groups)
    pieces, (cot_ref, base_ref) = refs[:n], refs[n : n + 2]
    total = base_ref[...].astype(F32)
    at = 0
    for size in groups:
        left, right = [], []
        for i in range(at, at + size):
            left.append(pieces[i][...])
            rows = pieces[i].shape[0]
            right.append(cot_ref[pl.ds(pl.multiple_of(starts_ref[i], rows), rows), :])
        at += size
        total = total + mm(jnp.concatenate(left, 0), jnp.concatenate(right, 0), 0, 0)
    if final:
        basis_ref, factor_ref, out_ref = refs[n + 2 :]
        total = total - mm(basis_ref[...], factor_ref[...], 0, 0)
    else:
        (out_ref,) = refs[n + 2 :]
    out_ref[...] = total.astype(out_ref.dtype)


def grad_call(pieces, groups, starts, cot, base, low_rank, tile):
    d, cols = base.shape
    final = low_rank is not None
    in_specs = [pl.BlockSpec((p.shape[0], tile), lambda i, s: (0, i)) for p in pieces]
    in_specs += [pl.BlockSpec(cot.shape, lambda i, s: (0, 0)), pl.BlockSpec((tile, cols), lambda i, s: (i, 0))]
    args = list(pieces) + [cot, base]
    k = sum(p.shape[0] for p in pieces)
    if final:
        basis, factor = low_rank
        in_specs += [pl.BlockSpec((basis.shape[0], tile), lambda i, s: (0, i)), pl.BlockSpec(factor.shape, lambda i, s: (0, 0))]
        args += [basis, factor]
        k += basis.shape[0]
    out = jax.ShapeDtypeStruct((d, cols), BF16 if final else F32)
    return pl.pallas_call(
        functools.partial(grad_kernel, tuple(groups), final),
        out_shape=out,
        grid_spec=pltpu.PrefetchScalarGridSpec(
            num_scalar_prefetch=1,
            grid=(d // tile,),
            in_specs=in_specs,
            out_specs=pl.BlockSpec((tile, cols), lambda i, s: (i, 0)),
        ),
        compiler_params=pltpu.CompilerParams(vmem_limit_bytes=VMEM_LIMIT),
        cost_estimate=pl.CostEstimate(flops=2 * d * cols * k, bytes_accessed=2 * d * k + 6 * d * cols, transcendentals=0),
        name="gradient_final" if final else "gradient_part",
    )(starts, *args)


def input_kernel(n_cot, n_w, quarter_ref, *refs):
    cots, refs = refs[:n_cot], refs[n_cot:]
    own_ref, sib_ref, refs = refs[0], refs[1], refs[2:]
    w_own, w_sib, out_ref = refs[:n_w], refs[n_w : 2 * n_w], refs[2 * n_w]
    tokens = jnp.concatenate([c[...] for c in cots], 0)
    wide = 2 * own_ref.shape[1]
    total = mm(tokens[:, :wide], jnp.concatenate([own_ref[...], sib_ref[...]], 1), 1, 1)
    for s in range(w_own[0].shape[0]):
        rows = [jnp.concatenate([o[s], b[s]], 1) for o, b in zip(w_own, w_sib)]
        total = total + mm(tokens[:, (s + 1) * wide : (s + 2) * wide], jnp.concatenate(rows, 0), 1, 1)
    out_ref[...] = total.astype(BF16)


def input_call(cots, own, sib, where, w_own, w_sib):
    rows = sum(w.shape[1] for w in w_own)
    cols = own.shape[1]
    tokens = sum(c.shape[0] for c in cots)
    whole = lambda a: pl.BlockSpec(a.shape, lambda i, q, n=a.ndim: (0,) * n)
    spec = pl.BlockSpec((rows, cols), lambda i, q: (q[0], 0))
    return pl.pallas_call(
        functools.partial(input_kernel, len(cots), len(w_own)),
        out_shape=jax.ShapeDtypeStruct((tokens, rows), BF16),
        grid_spec=pltpu.PrefetchScalarGridSpec(
            num_scalar_prefetch=1,
            grid=(1,),
            in_specs=[whole(c) for c in cots] + [spec, spec] + [whole(w) for w in w_own + w_sib],
            out_specs=pl.BlockSpec((tokens, rows), lambda i, q: (0, 0)),
        ),
        compiler_params=pltpu.CompilerParams(vmem_limit_bytes=VMEM_LIMIT),
        cost_estimate=pl.CostEstimate(
            flops=2 * tokens * rows * cols * 8, bytes_accessed=16 * cols * (tokens + rows) + 2 * tokens * rows, transcendentals=0
        ),
        name="input_grads_part",
    )(jnp.reshape(where, (1,)).astype(jnp.int32), *cots, own, sib, *w_own, *w_sib)


def place_kernel(at_ref, *refs):
    ins, out_ref = refs[:-1], refs[-1]
    k = 0
    for ref in ins:
        for j in range(ref.shape[0]):
            width = ref.shape[2]
            out_ref[:, pl.ds(pl.multiple_of(at_ref[k] * width, 128), width)] = ref[j]
            k += 1


def place_call(pieces, at):
    tokens, width = pieces[0].shape[1:]
    total = width * sum(p.shape[0] for p in pieces)
    return pl.pallas_call(
        place_kernel,
        out_shape=jax.ShapeDtypeStruct((tokens, total), BF16),
        grid_spec=pltpu.PrefetchScalarGridSpec(
            num_scalar_prefetch=1,
            grid=(1,),
            in_specs=[pl.BlockSpec(p.shape, lambda i, a: (0, 0, 0)) for p in pieces],
            out_specs=pl.BlockSpec((tokens, total), lambda i, a: (0, 0)),
        ),
        compiler_params=pltpu.CompilerParams(vmem_limit_bytes=VMEM_LIMIT),
        cost_estimate=pl.CostEstimate(flops=0, bytes_accessed=4 * tokens * total, transcendentals=0),
        name="place_blocks",
    )(at.astype(jnp.int32), *pieces)


def per_device(activations, cotangent, weight, residual, warm_factor):
    iy, iz, ix, ic = (lax.axis_index(a) for a in ("y", "z", "x", "core"))
    tok, d = activations.shape
    tok_dev, cols = cotangent.shape
    rank = warm_factor.shape[1]
    residual = residual[0]
    scale = tok_dev ** (-0.5)
    quarter = d // 4
    sub = quarter // 4

    warm3 = jnp.concatenate(split3(warm_factor.T), 0)
    cw = fold3(mm(warm3, cotangent, 1, 1)) * scale
    cw = reduce_scatter(cw.reshape(rank, 4, 2 * tok).transpose(1, 0, 2), "x")
    cw = reduce_scatter(cw.reshape(rank, 2, tok).transpose(1, 0, 2), "core")

    cot_blocks = cotangent.reshape(4, 2, tok, cols)
    cot_mine = lax.dynamic_index_in_dim(cot_blocks, ic, 1, False)
    cot_sib = shift(lax.dynamic_index_in_dim(cot_blocks, 1 - ic, 1, False), "core", 1)
    w_quarter = lax.dynamic_slice_in_dim(weight, iz * quarter, quarter, 0)
    w_quarter_sib = shift(w_quarter, "core", 1)
    w_send = lax.dynamic_slice_in_dim(weight, iz * quarter + iy * sub, sub, 0)
    got = []
    for s in (1, 3, 2):
        to = (ix + s) % 4
        got.append((s, shift(jnp.concatenate([block(cot_mine, to), block(cot_sib, to), w_send], 0), "x", s)))
    got = [g for _, g in sorted(got, key=lambda p: p[0])]
    cot_own = jnp.concatenate(
        [block(cot_mine, ix), block(cot_sib, ix)] + [g[i * tok : (i + 1) * tok] for g in got for i in (0, 1)], 1
    )
    w_own = jnp.stack([g[2 * tok :] for g in got])

    half = tok // 2
    c_low, c_high, c_far_a, c_far_b = ring(cot_own, "z", (lambda v: v[:half], lambda v: v[half:]))
    hs = sub // 2
    w_low, w_high, w_far_a, w_far_b = ring(w_own, "y", (lambda v: v[:, :hs], lambda v: v[:, hs:]))

    act, _ = lax.optimization_barrier((activations, got[0]))
    a_low, a_high, a_far_a, a_far_b = ring(act, "x", (lambda v: v[:half], lambda v: v[half:]))
    a_sib = shift(activations, "core", 1)
    a_low_sib, a_high_sib, a_far_a_sib, a_far_b_sib = (shift(v, "core", 1) for v in (a_low, a_high, a_far_a, a_far_b))

    cw3 = jnp.concatenate(split3(cw), 0)
    left = fold3(mm(cw3, activations, 1, 0)) + fold3(mm(warm3, residual, 1, 1))
    tiles = left.reshape(rank // 8, 8, d // 128, 128).transpose(0, 2, 1, 3).reshape(-1, 8, 128)
    n_tiles = tiles.shape[0]
    part = reduce_scatter(tiles.reshape(2, n_tiles // 2, 8, 128), "core")
    part = reduce_scatter(part.reshape(4, n_tiles // 8, 8, 128), "y")
    part = reduce_scatter(part.reshape(4, n_tiles // 32, 8, 128), "z")
    part = all_sum(part, "x")
    part = all_blocks(part, "z").reshape(-1, 8, 128)
    part = all_blocks(part, "y").reshape(-1, 8, 128)
    part = all_blocks(part, "core")
    left = part.reshape(rank // 8, d // 128, 8, 128).transpose(0, 2, 1, 3).reshape(rank, d)

    left3 = jnp.concatenate(split3(left), 0)
    right = fold3(mm(left3, activations, 1, 1)) * scale
    right = all_blocks(right, "core").transpose(1, 0, 2).reshape(rank, 2 * tok)
    right = all_blocks(right, "x").transpose(1, 0, 2).reshape(rank, 8 * tok)
    right3 = jnp.concatenate(split3(right), 0)
    sums = fold3(mm(right3, cotangent, 1, 0)) + fold3(mm(left3, residual, 1, 0))
    sums = all_sum(all_sum(sums, "y"), "z")
    gram = mm(left3, left3, 1, 1).reshape(3, rank, 3, rank).sum((0, 2))
    inverse = inverse_of_factor(gram)
    basis = jnp.dot(inverse, left, precision=lax.Precision.HIGHEST)
    factor = jnp.dot(inverse, sums, precision=lax.Precision.HIGHEST) * (1.0 / 16)
    b_h, b_m, b_l = split3(basis)
    f_h, f_m, f_l = split3(factor)
    basis6 = jnp.concatenate([b_h, b_m, b_l, b_h, b_m, b_h], 0)
    factor6 = jnp.concatenate([f_h, f_h, f_h, f_m, f_m, f_l], 0)

    cots = [cot_own, c_low, c_high, c_far_a, c_far_b]
    w_sets = [[w_own], [w_low], [w_high], [w_far_a, w_far_b]]
    parts = []
    for step, w_set in zip((0, -1, 1, 2), w_sets):
        sib_set = [shift(w, "core", 1) for w in w_set]
        parts.append(input_call(cots, w_quarter, w_quarter_sib, (iy + step) % 4, w_set, sib_set))
    grads = jnp.stack([p.reshape(4, tok, sub) for p in parts], 1)
    back = [grads[0], shift(grads[1], "z", -1), shift(grads[2], "z", 1), shift(grads[3], "z", 2)]
    ys = jnp.stack([(iy + s) % 4 for s in (0, -1, 1, 2)])
    at = jnp.concatenate([((iz + s) % 4) * 4 + ys for s in (0, 1, -1, 2)])
    input_grads = place_call(back, at)

    cot_scaled = (cotangent.astype(F32) * scale).astype(BF16)

    def start(step, sib):
        return ((ix + step) % 4) * 2 * tok + (1 - ic if sib else ic) * tok

    near = [activations, a_sib, a_low, a_low_sib, a_high, a_high_sib]
    starts = jnp.stack([start(s, b) for s in (0, -1, 1) for b in (False, True)]).astype(jnp.int32)
    merged = grad_call(near, (2, 2, 2), starts, cot_scaled, residual, None, 512)
    far = [a_far_a, a_far_b, a_far_a_sib, a_far_b_sib]
    starts = jnp.stack([start(2, b) + h for b in (False, True) for h in (0, half)]).astype(jnp.int32)
    new_residual = grad_call(far, (4,), starts, cot_scaled, merged, (basis6, factor6), 512)
    return factor.T, new_residual[None], input_grads


def solution(mesh):
    fine = Mesh(mesh.devices.reshape(4, 4, 4, 2), ("y", "z", "x", "core"))
    dp, tensor = ("y", "z"), ("x", "core")
    in_specs = (
        P(dp + tensor, None),
        P(dp, tensor),
        P(None, tensor),
        P(dp, None, tensor),
        P(tensor, None),
    )
    out_specs = (P(tensor, None), P(dp, None, tensor), P(dp + tensor, None))
    return jax.shard_map(per_device, mesh=fine, in_specs=in_specs, out_specs=out_specs, check_vma=False)
```

```python
import functools
import math

import jax
import jax.numpy as jnp
from jax import lax
from jax.experimental import pallas as pl
from jax.experimental.pallas import tpu as pltpu
from jax.sharding import Mesh, PartitionSpec as P

BF16, F32 = jnp.bfloat16, jnp.float32
SIZE = {"y": 4, "z": 4, "x": 4, "core": 2}
VMEM_LIMIT = 56 * 1024 * 1024


def shift(value, axis, step):
    n = SIZE[axis]
    return lax.ppermute(value, axis, [(i, (i + step) % n) for i in range(n)])


def split3(value):
    high = lax.reduce_precision(value, 8, 7)
    rest = value - high
    mid = lax.reduce_precision(rest, 8, 7)
    return high.astype(BF16), mid.astype(BF16), (rest - mid).astype(BF16)


def fold3(value):
    rows = value.shape[0] // 3
    return value[:rows] + value[rows : 2 * rows] + value[2 * rows :]


def mm(a, b, ca, cb):
    return lax.dot_general(a, b, (((ca,), (cb,)), ((), ())), preferred_element_type=F32)


def block(value, index):
    return lax.dynamic_index_in_dim(value, index, 0, False)


def reduce_scatter(value, axis):
    n, me = SIZE[axis], lax.axis_index(axis)
    parts = [shift(block(value, (me + s) % n), axis, s) for s in range(1, n)]
    total = block(value, me)
    for part in parts:
        total = total + part
    return total


def all_sum(value, axis):
    parts = [shift(value, axis, s) for s in range(1, SIZE[axis])]
    for part in parts:
        value = value + part
    return value


def all_blocks(value, axis):
    n = math.prod(SIZE[a] for a in axis)
    return lax.all_to_all(jnp.broadcast_to(value[None], (n,) + value.shape), axis, 0, 0)


def both_cores(value):
    other = shift(value, "core", 1)
    first = lax.axis_index("core") == 0
    return jnp.stack([jnp.where(first, value, other), jnp.where(first, other, value)])


def inverse_kernel(left_ref, out_ref):
    n = out_ref.shape[0]
    grams = mm(left_ref[...], left_ref[...], 1, 1)
    gram = fold3(grams[:, :n] + grams[:, n : 2 * n] + grams[:, 2 * n :])
    row = lax.broadcasted_iota(jnp.int32, (n, 2 * n), 0)
    col = lax.broadcasted_iota(jnp.int32, (n, 2 * n), 1)
    eye = jnp.where(row + n == col, 1.0, 0.0).astype(F32)
    work = jnp.concatenate([gram, jnp.zeros((n, n), F32)], axis=1) + eye
    for k in range(n):
        pivot_row = work[k : k + 1, :]
        pivot = jnp.sum(jnp.where(col[:1] == k, pivot_row, 0.0), axis=1, keepdims=True)
        column = jnp.sum(jnp.where(col == k, work, 0.0), axis=1, keepdims=True)
        factor = jnp.where(row[:, :1] > k, column / pivot, 0.0)
        root = lax.rsqrt(pivot)
        root = root * (1.5 - 0.5 * pivot * root * root)
        scale = jnp.where(row[:, :1] == k, root, 1.0)
        work = (work - factor * pivot_row) * scale
    out_ref[...] = work[:, n:]


def inverse_of_factor(left3):
    rank = left3.shape[0] // 3
    return pl.pallas_call(
        inverse_kernel,
        out_shape=jax.ShapeDtypeStruct((rank, rank), F32),
        name="inverse_of_factor",
    )(left3)


def parts3(value):
    high = value.astype(BF16)
    rest = value - high.astype(F32)
    mid = rest.astype(BF16)
    return high, mid, (rest - mid.astype(F32)).astype(BF16)


def residual_kernel(act_ref, cot_ref, residual_ref, left_ref, inverse_ref, factor_ref, out_ref):
    basis = lax.dot_general(
        inverse_ref[...], left_ref[...], (((1,), (0,)), ((), ())), precision=lax.Precision.HIGHEST, preferred_element_type=F32
    )
    b_h, b_m, b_l = parts3(basis)
    f_h, f_m, f_l = parts3(factor_ref[...])
    basis6 = jnp.concatenate([b_h, b_m, b_l, b_h, b_m, b_h], 0)
    factor6 = jnp.concatenate([f_h, f_h, f_h, f_m, f_m, f_l], 0)
    total = mm(act_ref[...], cot_ref[...], 0, 0) + residual_ref[...].astype(F32)
    out_ref[...] = (total - mm(basis6, factor6, 0, 0)).astype(BF16)


def residual_call(act, cot, residual, left, inverse, factor, tile):
    k, d = act.shape
    cols, rank = cot.shape[1], left.shape[0]
    whole = lambda a: pl.BlockSpec(a.shape, lambda i: (0, 0))
    rows = pl.BlockSpec((tile, cols), lambda i: (i, 0))
    return pl.pallas_call(
        residual_kernel,
        out_shape=jax.ShapeDtypeStruct((d, cols), BF16),
        grid=(d // tile,),
        in_specs=[
            pl.BlockSpec((k, tile), lambda i: (0, i)),
            whole(cot),
            rows,
            pl.BlockSpec((rank, tile), lambda i: (0, i)),
            whole(inverse),
            whole(factor),
        ],
        out_specs=rows,
        compiler_params=pltpu.CompilerParams(vmem_limit_bytes=VMEM_LIMIT),
        cost_estimate=pl.CostEstimate(
            flops=2 * d * cols * (k + 6 * rank), bytes_accessed=2 * d * k + 4 * d * cols + 4 * d * rank, transcendentals=0
        ),
        name="new_residual",
    )(act, cot, residual, left, inverse, factor)


def input_kernel(n_cot, at_ref, *refs):
    cots, w_ref, outs = refs[:n_cot], refs[n_cot], refs[n_cot + 1 :]
    blocks, chips, cores = w_ref.shape[:3]
    tok, width = outs[0].shape
    total = jnp.zeros((tok * len(outs), width), F32)
    for s in range(chips):
        tokens = jnp.concatenate([jnp.concatenate([c[2 * s], c[2 * s + 1]], 1) for c in cots], 0)
        rows = [jnp.concatenate([w_ref[b, at_ref[s], at_ref[chips + c]] for c in range(cores)], 1) for b in range(blocks)]
        total = total + mm(tokens, jnp.concatenate(rows, 0), 1, 1)
    for i, out in enumerate(outs):
        out[...] = total[i * tok : (i + 1) * tok].astype(BF16)


def input_call(cots, weight, at, blocks):
    n, chips, cores, rows, cols = weight.shape
    _, tok, _ = cots[0].shape
    tokens = 4 * tok
    return pl.pallas_call(
        functools.partial(input_kernel, len(cots)),
        out_shape=[jax.ShapeDtypeStruct((tok, n * rows), BF16)] * 4,
        grid_spec=pltpu.PrefetchScalarGridSpec(
            num_scalar_prefetch=1,
            grid=(n // blocks,),
            in_specs=[pl.BlockSpec(c.shape, lambda i, q: (0, 0, 0)) for c in cots]
            + [pl.BlockSpec((blocks, chips, cores, rows, cols), lambda i, q: (i, 0, 0, 0, 0))],
            out_specs=[pl.BlockSpec((tok, blocks * rows), lambda i, q: (0, i))] * 4,
        ),
        compiler_params=pltpu.CompilerParams(vmem_limit_bytes=VMEM_LIMIT),
        cost_estimate=pl.CostEstimate(
            flops=2 * tokens * n * rows * cols * 8, bytes_accessed=16 * cols * (tokens + n * rows), transcendentals=0
        ),
        name="input_grads",
    )(jnp.stack(at).astype(jnp.int32), *cots, weight)


def copy_kernel(n_in, n_out, plan, at_ref, *refs):
    ins, outs, sems = refs[:n_in], refs[n_in : n_in + n_out], refs[n_in + n_out]
    copies = [pltpu.make_async_copy(*pair, sems.at[i]) for i, pair in enumerate(plan(at_ref, ins, outs))]
    for copy in copies:
        copy.start()
    for copy in copies:
        copy.wait()


def copy_call(plan, n_copies, ins, outs, at, name):
    any_spec = pl.BlockSpec(memory_space=pl.ANY)
    moved = sum(2 * math.prod(o.shape) * o.dtype.itemsize for o in outs)
    return pl.pallas_call(
        functools.partial(copy_kernel, len(ins), len(outs), plan),
        out_shape=outs,
        grid_spec=pltpu.PrefetchScalarGridSpec(
            num_scalar_prefetch=1,
            grid=(1,),
            in_specs=[any_spec] * len(ins),
            out_specs=[pl.BlockSpec(o.shape, lambda i, a, n=len(o.shape): (0,) * n) for o in outs],
            scratch_shapes=[pltpu.SemaphoreType.DMA((n_copies,))],
        ),
        compiler_params=pltpu.CompilerParams(vmem_limit_bytes=VMEM_LIMIT),
        cost_estimate=pl.CostEstimate(flops=0, bytes_accessed=moved, transcendentals=0),
        name=name,
    )(jnp.stack(at).astype(jnp.int32), *ins)


def part_of(ref, index, size):
    return ref.at[pl.ds(pl.multiple_of(index * size, size), size)]


def pack_plan(tok, at, ins, outs):
    return [
        (part_of(cot, at[s], tok), out.at[pl.ds(i * tok, tok)]) for s, out in zip((1, 2, 3), outs) for i, cot in enumerate(ins)
    ]


def unpack_plan(tok, at, ins, outs):
    cot, other, *got = ins
    pairs = [(part_of(cot, at[0], tok), outs[0].at[0]), (part_of(other, at[0], tok), outs[0].at[1])]
    return pairs + [(g.at[pl.ds(i * tok, tok)], outs[0].at[2 * s + 2 + i]) for s, g in enumerate(got) for i in (0, 1)]


def place_plan(width, at, ins, outs):
    return [(r, outs[0].at[:, pl.ds(pl.multiple_of(at[i] * width, width), width)]) for i, r in enumerate(ins)]


def per_device(activations, cotangent, weight, residual, warm_factor):
    iy, iz, ix, ic = (lax.axis_index(a) for a in ("y", "z", "x", "core"))
    tok, d = activations.shape
    tok_dev, cols = cotangent.shape
    rank = warm_factor.shape[1]
    residual = residual[0]
    scale = tok_dev ** (-0.5)
    quarter = d // 4
    sub = quarter // 4

    like = lambda *shape: jax.ShapeDtypeStruct(shape, BF16)
    w_send = lax.dynamic_slice_in_dim(weight, iz * quarter + iy * sub, sub, 0)
    w_all = lax.all_gather(w_send, ("y", "x", "core")).reshape(4, 4, 2, sub, cols)

    cot_other = shift(cotangent, "core", 1)
    at = [((ix + s) % 4) * 2 + ic for s in range(4)]
    packed = copy_call(functools.partial(pack_plan, tok), 6, [cotangent, cot_other], [like(2 * tok, cols)] * 3, at, "pack")
    got = [shift(p, "x", s) for s, p in zip((1, 2, 3), packed)]

    cot, w_send, *_ = lax.optimization_barrier((cotangent, w_send, *packed))
    warm3 = jnp.concatenate(split3(warm_factor.T), 0)
    cw = fold3(mm(warm3, cot, 1, 1)) * scale
    cw = reduce_scatter(cw.reshape(rank, 4, 2 * tok).transpose(1, 0, 2), "x")
    act, cw = lax.optimization_barrier((activations, cw))
    gathered = lax.all_gather(act, ("x", "core"), axis=0, tiled=True)
    cw = reduce_scatter(cw.reshape(rank, 2, tok).transpose(1, 0, 2), "core")

    cw3 = jnp.concatenate(split3(cw), 0)
    left = fold3(mm(cw3, activations, 1, 0)) + fold3(mm(warm3, residual, 1, 1))
    tiles = left.reshape(rank // 8, 8, d // 128, 128).transpose(0, 2, 1, 3).reshape(-1, 8, 128)
    n_tiles = tiles.shape[0]
    part = reduce_scatter(tiles.reshape(2, n_tiles // 2, 8, 128), "core")
    part = lax.all_to_all(part.reshape(16, n_tiles // 32, 8, 128), ("y", "z"), 0, 0).sum(0)
    part, *got = lax.optimization_barrier((part, *got))

    (cot_own,) = copy_call(
        functools.partial(unpack_plan, tok), 8, [cotangent, cot_other] + got, [like(8, tok, cols)], at, "unpack"
    )
    c_low, c_high = shift(cot_own, "z", 1), shift(cot_own, "z", -1)
    part = all_blocks(part, ("x",)).sum(0)
    part, cot_own = lax.optimization_barrier((part, cot_own))
    part = all_blocks(part, ("y", "z")).reshape(-1, 8, 128)
    part, c_low, c_high = lax.optimization_barrier((part, c_low, c_high))
    half = tok // 2
    c_far = [shift(c_low[:, :half], "z", 1), shift(c_high[:, half:], "z", -1)]
    part = both_cores(part)
    left = part.reshape(rank // 8, d // 128, 8, 128).transpose(0, 2, 1, 3).reshape(rank, d)

    left3 = jnp.concatenate(split3(left), 0)
    right = fold3(mm(left3, activations, 1, 1)) * scale
    right = all_blocks(both_cores(right), ("x",))

    right, *c_far = lax.optimization_barrier((right, *c_far))
    cots = [cot_own, c_low, c_high, *c_far]
    grads = input_call(cots, w_all, [(ix - s) % 4 for s in range(4)] + [ic, 1 - ic], 2)
    right, *grads = lax.optimization_barrier((right, *grads))
    back = [grads[0], shift(grads[1], "z", -1), shift(grads[2], "z", 1), shift(grads[3], "z", 2)]

    right = right.reshape(8, rank, tok).transpose(1, 0, 2).reshape(rank, 8 * tok)
    right3 = jnp.concatenate(split3(right), 0)
    sums = fold3(mm(right3, cotangent, 1, 0)) + fold3(mm(left3, residual, 1, 0))
    sums = all_sum(sums, "y")
    at = [(iz + s) % 4 for s in (0, 1, -1, 2)]
    (input_grads,) = copy_call(functools.partial(place_plan, quarter), 4, back, [like(tok, d)], at, "place")
    sums = all_sum(sums, "z")
    left3, right = lax.optimization_barrier((left3, right))
    inverse = inverse_of_factor(left3)
    factor = jnp.dot(inverse, sums, precision=lax.Precision.HIGHEST) * (1.0 / 16)
    cot_scaled = (cotangent.astype(F32) * scale).astype(BF16)
    new_residual = residual_call(gathered, cot_scaled, residual, left, inverse, factor, 1024)
    return factor.T, new_residual[None], input_grads


def solution(mesh):
    fine = Mesh(mesh.devices.reshape(4, 4, 4, 2), ("y", "z", "x", "core"))
    dp, tensor = ("y", "z"), ("x", "core")
    in_specs = (
        P(dp + tensor, None),
        P(dp, tensor),
        P(None, tensor),
        P(dp, None, tensor),
        P(tensor, None),
    )
    out_specs = (P(tensor, None), P(dp, None, tensor), P(dp + tensor, None))
    return jax.shard_map(per_device, mesh=fine, in_specs=in_specs, out_specs=out_specs, check_vma=False)
```

```python
import functools
import math

import jax
import jax.numpy as jnp
from jax import lax
from jax.experimental import pallas as pl
from jax.experimental.pallas import tpu as pltpu
from jax.sharding import Mesh, PartitionSpec as P

BF16, F32 = jnp.bfloat16, jnp.float32
SIZE = {"y": 4, "z": 4, "x": 4, "core": 2}
VMEM_LIMIT = 56 * 1024 * 1024


def shift(value, axis, step):
    n = SIZE[axis]
    return lax.ppermute(value, axis, [(i, (i + step) % n) for i in range(n)])


def split3(value):
    high = lax.reduce_precision(value, 8, 7)
    rest = value - high
    mid = lax.reduce_precision(rest, 8, 7)
    return high.astype(BF16), mid.astype(BF16), (rest - mid).astype(BF16)


def parts3(value):
    high = value.astype(BF16)
    rest = value - high.astype(F32)
    mid = rest.astype(BF16)
    return high, mid, (rest - mid.astype(F32)).astype(BF16)


def fold3(value):
    rows = value.shape[0] // 3
    return value[:rows] + value[rows : 2 * rows] + value[2 * rows :]


def mm(a, b, ca, cb):
    return lax.dot_general(a, b, (((ca,), (cb,)), ((), ())), preferred_element_type=F32)


def block(value, index):
    return lax.dynamic_index_in_dim(value, index, 0, False)


def reduce_scatter(value, axis):
    n, me = SIZE[axis], lax.axis_index(axis)
    parts = [shift(block(value, (me + s) % n), axis, s) for s in range(1, n)]
    total = block(value, me)
    for part in parts:
        total = total + part
    return total


def all_sum(value, axis):
    parts = [shift(value, axis, s) for s in range(1, SIZE[axis])]
    for part in parts:
        value = value + part
    return value


def all_blocks(value, axis):
    n = math.prod(SIZE[a] for a in axis)
    return lax.all_to_all(jnp.broadcast_to(value[None], (n,) + value.shape), axis, 0, 0)


def both_cores(value):
    other = shift(value, "core", 1)
    first = lax.axis_index("core") == 0
    return jnp.stack([jnp.where(first, value, other), jnp.where(first, other, value)])


def inverse_kernel(left_ref, out_ref):
    n = out_ref.shape[0]
    left3 = jnp.concatenate(parts3(left_ref[...]), 0)
    grams = mm(left3, left3, 1, 1)
    gram = fold3(grams[:, :n] + grams[:, n : 2 * n] + grams[:, 2 * n :])
    row = lax.broadcasted_iota(jnp.int32, (n, 2 * n), 0)
    col = lax.broadcasted_iota(jnp.int32, (n, 2 * n), 1)
    eye = jnp.where(row + n == col, 1.0, 0.0).astype(F32)
    work = jnp.concatenate([gram, jnp.zeros((n, n), F32)], axis=1) + eye
    for k in range(n - 1):
        pivot_row = work[k : k + 1, :]
        pivot = jnp.sum(jnp.where(col[:1] == k, pivot_row, 0.0), axis=1, keepdims=True)
        column = jnp.sum(jnp.where(col == k, work, 0.0), axis=1, keepdims=True)
        work = work - jnp.where(row[:, :1] > k, column / pivot, 0.0) * pivot_row
    pivots = jnp.sum(jnp.where(row == col, work, 0.0), axis=1, keepdims=True)
    root = lax.rsqrt(pivots)
    root = root * (1.5 - 0.5 * pivots * root * root)
    out_ref[...] = work[:, n:] * root


def inverse_of_factor(left):
    rank = left.shape[0]
    return pl.pallas_call(
        inverse_kernel,
        out_shape=jax.ShapeDtypeStruct((rank, rank), F32),
        name="inverse_of_factor",
    )(left)


def residual_kernel(scale, act_ref, cot_ref, residual_ref, left_ref, inverse_ref, factor_ref, out_ref):
    basis = lax.dot_general(
        inverse_ref[...], left_ref[...], (((1,), (0,)), ((), ())), precision=lax.Precision.HIGHEST, preferred_element_type=F32
    )
    b_h, b_m, b_l = parts3(basis)
    f_h, f_m, f_l = parts3(factor_ref[...])
    basis6 = jnp.concatenate([b_h, b_m, b_l, b_h, b_m, b_h], 0)
    factor6 = jnp.concatenate([f_h, f_h, f_h, f_m, f_m, f_l], 0)
    total = mm(act_ref[...], cot_ref[...], 0, 0) * scale + residual_ref[...].astype(F32)
    out_ref[...] = (total - mm(basis6, factor6, 0, 0)).astype(BF16)


def residual_call(scale, act, cot, residual, left, inverse, factor, tile):
    k, d = act.shape
    cols, rank = cot.shape[1], left.shape[0]
    whole = lambda a: pl.BlockSpec(a.shape, lambda i: (0, 0))
    rows = pl.BlockSpec((tile, cols), lambda i: (i, 0))
    return pl.pallas_call(
        functools.partial(residual_kernel, scale),
        out_shape=jax.ShapeDtypeStruct((d, cols), BF16),
        grid=(d // tile,),
        in_specs=[
            pl.BlockSpec((k, tile), lambda i: (0, i)),
            whole(cot),
            rows,
            pl.BlockSpec((rank, tile), lambda i: (0, i)),
            whole(inverse),
            whole(factor),
        ],
        out_specs=rows,
        compiler_params=pltpu.CompilerParams(vmem_limit_bytes=52 * 1024 * 1024),
        cost_estimate=pl.CostEstimate(
            flops=2 * d * cols * (k + 6 * rank), bytes_accessed=2 * d * k + 4 * d * cols + 4 * d * rank, transcendentals=0
        ),
        name="new_residual",
    )(act, cot, residual, left, inverse, factor)


def input_kernel(n_cot, at_ref, *refs):
    cots, weights, outs = refs[:n_cot], refs[n_cot : n_cot + 2], refs[n_cot + 2 :]
    blocks, chips = weights[0].shape[:2]
    tok, width = outs[0].shape
    total = jnp.zeros((tok * len(outs), width), F32)
    for s in range(chips):
        tokens = jnp.concatenate([jnp.concatenate([c[2 * s], c[2 * s + 1]], 1) for c in cots], 0)
        rows = [jnp.concatenate([w[b, at_ref[4 + s]] for w in weights], 1) for b in range(blocks)]
        total = total + mm(tokens, jnp.concatenate(rows, 0), 1, 1)
    for i, out in enumerate(outs):
        out[...] = total[i * tok : (i + 1) * tok].astype(BF16)


def input_call(cots, weight, other, at, blocks):
    n, chips, rows, cols = weight.shape
    _, tok, _ = cots[0].shape
    tokens = 4 * tok
    return pl.pallas_call(
        functools.partial(input_kernel, len(cots)),
        out_shape=[jax.ShapeDtypeStruct((tok, n * rows), BF16)] * 4,
        grid_spec=pltpu.PrefetchScalarGridSpec(
            num_scalar_prefetch=1,
            grid=(n // blocks,),
            in_specs=[pl.BlockSpec(c.shape, lambda i, q: (0, 0, 0)) for c in cots]
            + [pl.BlockSpec((blocks, chips, rows, cols), lambda i, q: (i, 0, 0, 0))] * 2,
            out_specs=[pl.BlockSpec((tok, blocks * rows), lambda i, q: (0, i))] * 4,
        ),
        compiler_params=pltpu.CompilerParams(vmem_limit_bytes=VMEM_LIMIT),
        cost_estimate=pl.CostEstimate(
            flops=2 * tokens * n * rows * cols * 8, bytes_accessed=16 * cols * (tokens + n * rows), transcendentals=0
        ),
        name="input_grads",
    )(at, *cots, weight, other)


def copy_kernel(n_in, n_out, plan, at_ref, *refs):
    ins, outs, sems = refs[:n_in], refs[n_in : n_in + n_out], refs[n_in + n_out]
    copies = [pltpu.make_async_copy(*pair, sems.at[i]) for i, pair in enumerate(plan(at_ref, ins, outs))]
    for copy in copies:
        copy.start()
    for copy in copies:
        copy.wait()


def copy_call(plan, n_copies, ins, outs, at, name):
    any_spec = pl.BlockSpec(memory_space=pl.ANY)
    moved = sum(2 * math.prod(o.shape) * o.dtype.itemsize for o in outs)
    return pl.pallas_call(
        functools.partial(copy_kernel, len(ins), len(outs), plan),
        out_shape=outs,
        grid_spec=pltpu.PrefetchScalarGridSpec(
            num_scalar_prefetch=1,
            grid=(1,),
            in_specs=[any_spec] * len(ins),
            out_specs=[pl.BlockSpec(o.shape, lambda i, a, n=len(o.shape): (0,) * n) for o in outs],
            scratch_shapes=[pltpu.SemaphoreType.DMA((n_copies,))],
        ),
        compiler_params=pltpu.CompilerParams(vmem_limit_bytes=VMEM_LIMIT),
        cost_estimate=pl.CostEstimate(flops=0, bytes_accessed=moved, transcendentals=0),
        name=name,
    )(at, *ins)


def part_of(ref, index, size):
    return ref.at[pl.ds(pl.multiple_of(index * size, size), size)]


def pack_plan(tok, at, ins, outs):
    return [
        (part_of(cot, at[s], tok), out.at[pl.ds(i * tok, tok)]) for s, out in zip((1, 2, 3), outs) for i, cot in enumerate(ins)
    ]


def unpack_plan(tok, at, ins, outs):
    cot, other, *got = ins
    pairs = [(part_of(cot, at[0], tok), outs[0].at[0]), (part_of(other, at[0], tok), outs[0].at[1])]
    return pairs + [(g.at[pl.ds(i * tok, tok)], outs[0].at[2 * s + 2 + i]) for s, g in enumerate(got) for i in (0, 1)]


def place_plan(width, at, ins, outs):
    return [(r, outs[0].at[:, pl.ds(pl.multiple_of(at[8 + i] * width, width), width)]) for i, r in enumerate(ins)]


def per_device(activations, cotangent, weight, residual, warm_factor):
    iy, iz, ix, ic = (lax.axis_index(a) for a in ("y", "z", "x", "core"))
    tok, d = activations.shape
    tok_dev, cols = cotangent.shape
    rank = warm_factor.shape[1]
    residual = residual[0]
    scale = tok_dev ** (-0.5)
    quarter = d // 4
    sub = quarter // 4

    like = lambda *shape: jax.ShapeDtypeStruct(shape, BF16)
    w_send = lax.dynamic_slice_in_dim(weight, iz * quarter + iy * sub, sub, 0)
    w_all = lax.all_gather(w_send, ("y", "x")).reshape(4, 4, sub, cols)

    cot_other = shift(cotangent, "core", 1)
    at = [((ix + s) % 4) * 2 + ic for s in range(4)] + [(ix - s) % 4 for s in range(4)]
    at = jnp.stack(at + [(iz + s) % 4 for s in (0, 1, -1, 2)]).astype(jnp.int32)
    packed = copy_call(functools.partial(pack_plan, tok), 6, [cotangent, cot_other], [like(2 * tok, cols)] * 3, at, "pack")

    warm3 = jnp.concatenate(split3(warm_factor.T), 0)
    cw = fold3(mm(warm3, cotangent, 1, 1)) * scale
    cw = reduce_scatter(cw.reshape(rank, 4, 2 * tok).transpose(1, 0, 2), "x")
    act, cw, *packed = lax.optimization_barrier((activations, cw, *packed))
    got = [shift(p, "x", s) for s, p in zip((1, 2, 3), packed)]
    gathered = lax.all_gather(act, ("x", "core"), axis=0, tiled=True)
    cw = reduce_scatter(cw.reshape(rank, 2, tok).transpose(1, 0, 2), "core")

    cw3 = jnp.concatenate(split3(cw), 0)
    left = fold3(mm(cw3, activations, 1, 0)) + fold3(mm(warm3, residual, 1, 1))
    tiles = left.reshape(rank // 8, 8, d // 128, 128).transpose(0, 2, 1, 3).reshape(-1, 8, 128)
    n_tiles = tiles.shape[0]
    part = reduce_scatter(tiles.reshape(2, n_tiles // 2, 8, 128), "core")
    part, *got = lax.optimization_barrier((part, *got))

    (cot_own,) = copy_call(
        functools.partial(unpack_plan, tok), 8, [cotangent, cot_other] + got, [like(8, tok, cols)], at, "unpack"
    )
    c_low, c_high = shift(cot_own, "z", 1), shift(cot_own, "z", -1)
    part = lax.all_to_all(part.reshape(16, n_tiles // 32, 8, 128), ("y", "z"), 0, 0).sum(0)
    part, c_low, c_high, w_all = lax.optimization_barrier((part, c_low, c_high, w_all))
    w_other = shift(w_all, "core", 1)
    half = tok // 2
    c_far = [shift(c_low[:, :half], "z", 1), shift(c_high[:, half:], "z", -1)]
    part = all_blocks(part, ("x",)).sum(0)
    part = all_blocks(part, ("y", "z")).reshape(-1, 8, 128)
    grads = input_call([cot_own, c_low, c_high, *c_far], w_all, w_other, at, 2)
    part, *grads = lax.optimization_barrier((part, *grads))
    back = [grads[0], shift(grads[1], "z", -1), shift(grads[2], "z", 1), shift(grads[3], "z", 2)]
    part = both_cores(part)
    left = part.reshape(rank // 8, d // 128, 8, 128).transpose(0, 2, 1, 3).reshape(rank, d)

    left3 = jnp.concatenate(split3(left), 0)
    right = fold3(mm(left3, activations, 1, 1)) * scale
    right = all_blocks(both_cores(right), ("x",))
    right = right.reshape(8, rank, tok).transpose(1, 0, 2).reshape(rank, 8 * tok)
    right3 = jnp.concatenate(split3(right), 0)
    sums = fold3(mm(right3, cotangent, 1, 0)) + fold3(mm(left3, residual, 1, 0))
    left, right = lax.optimization_barrier((left, right))
    inverse = inverse_of_factor(left)
    sums = all_sum(sums, "y")
    sums, inverse, *back = lax.optimization_barrier((sums, inverse, *back))
    (input_grads,) = copy_call(functools.partial(place_plan, quarter), 4, back, [like(tok, d)], at, "place")
    sums = all_sum(sums, "z")
    factor = jnp.dot(inverse, sums, precision=lax.Precision.HIGHEST) * (1.0 / 16)
    new_residual = residual_call(scale, gathered, cotangent, residual, left, inverse, factor, 1536 if d % 1536 == 0 else 1024)
    return factor.T, new_residual[None], input_grads


def solution(mesh):
    fine = Mesh(mesh.devices.reshape(4, 4, 4, 2), ("y", "z", "x", "core"))
    dp, tensor = ("y", "z"), ("x", "core")
    in_specs = (
        P(dp + tensor, None),
        P(dp, tensor),
        P(None, tensor),
        P(dp, None, tensor),
        P(tensor, None),
    )
    out_specs = (P(tensor, None), P(dp, None, tensor), P(dp + tensor, None))
    return jax.shard_map(per_device, mesh=fine, in_specs=in_specs, out_specs=out_specs, check_vma=False)
```

```python
import functools
import math

import jax
import jax.numpy as jnp
from jax import lax
from jax.experimental import pallas as pl
from jax.experimental.pallas import tpu as pltpu
from jax.sharding import Mesh, PartitionSpec as P

BF16, F32 = jnp.bfloat16, jnp.float32
SIZE = {"y": 4, "z": 4, "x": 4, "core": 2}
VMEM_LIMIT = 56 * 1024 * 1024


def shift(value, axis, step):
    n = SIZE[axis]
    return lax.ppermute(value, axis, [(i, (i + step) % n) for i in range(n)])


def split3(value):
    high = lax.reduce_precision(value, 8, 7)
    rest = value - high
    mid = lax.reduce_precision(rest, 8, 7)
    return high.astype(BF16), mid.astype(BF16), (rest - mid).astype(BF16)


def parts3(value):
    high = value.astype(BF16)
    rest = value - high.astype(F32)
    mid = rest.astype(BF16)
    return high, mid, (rest - mid.astype(F32)).astype(BF16)


def fold3(value):
    rows = value.shape[0] // 3
    return value[:rows] + value[rows : 2 * rows] + value[2 * rows :]


def mm(a, b, ca, cb):
    return lax.dot_general(a, b, (((ca,), (cb,)), ((), ())), preferred_element_type=F32)


def block(value, index):
    return lax.dynamic_index_in_dim(value, index, 0, False)


def reduce_scatter(value, axis):
    n, me = SIZE[axis], lax.axis_index(axis)
    parts = [shift(block(value, (me + s) % n), axis, s) for s in range(1, n)]
    total = block(value, me)
    for part in parts:
        total = total + part
    return total


def all_sum(value, axis):
    parts = [shift(value, axis, s) for s in range(1, SIZE[axis])]
    for part in parts:
        value = value + part
    return value


def all_blocks(value, axis):
    n = math.prod(SIZE[a] for a in axis)
    return lax.all_to_all(jnp.broadcast_to(value[None], (n,) + value.shape), axis, 0, 0)


def both_cores(value):
    other = shift(value, "core", 1)
    first = lax.axis_index("core") == 0
    return jnp.stack([jnp.where(first, value, other), jnp.where(first, other, value)])


def inverse_kernel(left_ref, out_ref):
    n = out_ref.shape[0]
    left3 = jnp.concatenate(parts3(left_ref[...]), 0)
    grams = mm(left3, left3, 1, 1)
    gram = fold3(grams[:, :n] + grams[:, n : 2 * n] + grams[:, 2 * n :])
    row = lax.broadcasted_iota(jnp.int32, (n, 2 * n), 0)
    col = lax.broadcasted_iota(jnp.int32, (n, 2 * n), 1)
    eye = jnp.where(row + n == col, 1.0, 0.0).astype(F32)
    work = jnp.concatenate([gram, jnp.zeros((n, n), F32)], axis=1) + eye
    for k in range(n - 1):
        pivot_row = work[k : k + 1, :]
        pivot = jnp.sum(jnp.where(col[:1] == k, pivot_row, 0.0), axis=1, keepdims=True)
        column = jnp.sum(jnp.where(col == k, work, 0.0), axis=1, keepdims=True)
        work = work - jnp.where(row[:, :1] > k, column / pivot, 0.0) * pivot_row
    pivots = jnp.sum(jnp.where(row == col, work, 0.0), axis=1, keepdims=True)
    root = lax.rsqrt(pivots)
    root = root * (1.5 - 0.5 * pivots * root * root)
    out_ref[...] = work[:, n:] * root


def inverse_of_factor(left):
    rank = left.shape[0]
    return pl.pallas_call(
        inverse_kernel,
        out_shape=jax.ShapeDtypeStruct((rank, rank), F32),
        name="inverse_of_factor",
    )(left)


def residual_kernel(scale, act_ref, cot_ref, residual_ref, left_ref, inverse_ref, factor_ref, out_ref):
    basis = lax.dot_general(
        inverse_ref[...], left_ref[...], (((1,), (0,)), ((), ())), precision=lax.Precision.HIGHEST, preferred_element_type=F32
    )
    b_h, b_m, b_l = parts3(basis)
    f_h, f_m, f_l = parts3(factor_ref[...])
    basis6 = jnp.concatenate([b_h, b_m, b_l, b_h, b_m, b_h], 0)
    factor6 = jnp.concatenate([f_h, f_h, f_h, f_m, f_m, f_l], 0)
    total = mm(act_ref[...], cot_ref[...], 0, 0) * scale + residual_ref[...].astype(F32)
    out_ref[...] = (total - mm(basis6, factor6, 0, 0)).astype(BF16)


def residual_call(scale, act, cot, residual, left, inverse, factor, tile):
    k, d = act.shape
    cols, rank = cot.shape[1], left.shape[0]
    whole = lambda a: pl.BlockSpec(a.shape, lambda i: (0, 0))
    rows = pl.BlockSpec((tile, cols), lambda i: (i, 0))
    return pl.pallas_call(
        functools.partial(residual_kernel, scale),
        out_shape=jax.ShapeDtypeStruct((d, cols), BF16),
        grid=(d // tile,),
        in_specs=[
            pl.BlockSpec((k, tile), lambda i: (0, i)),
            whole(cot),
            rows,
            pl.BlockSpec((rank, tile), lambda i: (0, i)),
            whole(inverse),
            whole(factor),
        ],
        out_specs=rows,
        compiler_params=pltpu.CompilerParams(vmem_limit_bytes=52 * 1024 * 1024),
        cost_estimate=pl.CostEstimate(
            flops=2 * d * cols * (k + 6 * rank), bytes_accessed=2 * d * k + 4 * d * cols + 4 * d * rank, transcendentals=0
        ),
        name="new_residual",
    )(act, cot, residual, left, inverse, factor)


def input_kernel(n_cot, at_ref, *refs):
    cots, weights, outs = refs[:n_cot], refs[n_cot : n_cot + 2], refs[n_cot + 2 :]
    blocks, chips = weights[0].shape[:2]
    tok, width = outs[0].shape
    total = jnp.zeros((tok * len(outs), width), F32)
    for s in range(chips):
        tokens = jnp.concatenate([jnp.concatenate([c[2 * s], c[2 * s + 1]], 1) for c in cots], 0)
        rows = [jnp.concatenate([w[b, at_ref[4 + s]] for w in weights], 1) for b in range(blocks)]
        total = total + mm(tokens, jnp.concatenate(rows, 0), 1, 1)
    for i, out in enumerate(outs):
        out[...] = total[i * tok : (i + 1) * tok].astype(BF16)


def input_call(cots, weight, other, at, blocks):
    n, chips, rows, cols = weight.shape
    _, tok, _ = cots[0].shape
    tokens = 4 * tok
    return pl.pallas_call(
        functools.partial(input_kernel, len(cots)),
        out_shape=[jax.ShapeDtypeStruct((tok, n * rows), BF16)] * 4,
        grid_spec=pltpu.PrefetchScalarGridSpec(
            num_scalar_prefetch=1,
            grid=(n // blocks,),
            in_specs=[pl.BlockSpec(c.shape, lambda i, q: (0, 0, 0)) for c in cots]
            + [pl.BlockSpec((blocks, chips, rows, cols), lambda i, q: (i, 0, 0, 0))] * 2,
            out_specs=[pl.BlockSpec((tok, blocks * rows), lambda i, q: (0, i))] * 4,
        ),
        compiler_params=pltpu.CompilerParams(vmem_limit_bytes=VMEM_LIMIT),
        cost_estimate=pl.CostEstimate(
            flops=2 * tokens * n * rows * cols * 8, bytes_accessed=16 * cols * (tokens + n * rows), transcendentals=0
        ),
        name="input_grads",
    )(at, *cots, weight, other)


def copy_kernel(n_in, n_out, plan, at_ref, *refs):
    ins, outs, sems = refs[:n_in], refs[n_in : n_in + n_out], refs[n_in + n_out]
    copies = [pltpu.make_async_copy(*pair, sems.at[i]) for i, pair in enumerate(plan(at_ref, ins, outs))]
    for copy in copies:
        copy.start()
    for copy in copies:
        copy.wait()


def copy_call(plan, n_copies, ins, outs, at, name):
    any_spec = pl.BlockSpec(memory_space=pltpu.HBM)
    moved = sum(2 * math.prod(o.shape) * o.dtype.itemsize for o in outs)
    return pl.pallas_call(
        functools.partial(copy_kernel, len(ins), len(outs), plan),
        out_shape=outs,
        grid_spec=pltpu.PrefetchScalarGridSpec(
            num_scalar_prefetch=1,
            grid=(1,),
            in_specs=[any_spec] * len(ins),
            out_specs=[pl.BlockSpec(o.shape, lambda i, a, n=len(o.shape): (0,) * n) for o in outs],
            scratch_shapes=[pltpu.SemaphoreType.DMA((n_copies,))],
        ),
        compiler_params=pltpu.CompilerParams(vmem_limit_bytes=VMEM_LIMIT),
        cost_estimate=pl.CostEstimate(flops=0, bytes_accessed=moved, transcendentals=0),
        name=name,
    )(at, *ins)


def part_of(ref, index, size):
    return ref.at[pl.ds(pl.multiple_of(index * size, size), size)]


def pack_plan(tok, at, ins, outs):
    return [
        (part_of(cot, at[s], tok), out.at[pl.ds(i * tok, tok)]) for s, out in zip((1, 2, 3), outs) for i, cot in enumerate(ins)
    ]


def unpack_plan(tok, at, ins, outs):
    cot, other, *got = ins
    pairs = [(part_of(cot, at[0], tok), outs[0].at[0]), (part_of(other, at[0], tok), outs[0].at[1])]
    return pairs + [(g.at[pl.ds(i * tok, tok)], outs[0].at[2 * s + 2 + i]) for s, g in enumerate(got) for i in (0, 1)]


def place_plan(width, at, ins, outs):
    return [(r, outs[0].at[:, pl.ds(pl.multiple_of(at[8 + i] * width, width), width)]) for i, r in enumerate(ins)]


def per_device(activations, cotangent, weight, residual, warm_factor):
    iy, iz, ix, ic = (lax.axis_index(a) for a in ("y", "z", "x", "core"))
    tok, d = activations.shape
    tok_dev, cols = cotangent.shape
    rank = warm_factor.shape[1]
    residual = residual[0]
    scale = tok_dev ** (-0.5)
    quarter = d // 4
    sub = quarter // 4

    like = lambda *shape: jax.ShapeDtypeStruct(shape, BF16)
    w_send = lax.dynamic_slice_in_dim(weight, iz * quarter + iy * sub, sub, 0)
    w_all = lax.all_gather(w_send, ("y", "x")).reshape(4, 4, sub, cols)

    cot_other = shift(cotangent, "core", 1)
    at = [((ix + s) % 4) * 2 + ic for s in range(4)] + [(ix - s) % 4 for s in range(4)]
    at = jnp.stack(at + [(iz + s) % 4 for s in (0, 1, -1, 2)]).astype(jnp.int32)
    packed = copy_call(functools.partial(pack_plan, tok), 6, [cotangent, cot_other], [like(2 * tok, cols)] * 3, at, "pack")

    warm3 = jnp.concatenate(split3(warm_factor.T), 0)
    cw = fold3(mm(warm3, cotangent, 1, 1)) * scale
    cw = reduce_scatter(cw.reshape(rank, 4, 2 * tok).transpose(1, 0, 2), "x")
    left = fold3(mm(warm3, residual, 1, 1))
    act, cw, left, *packed = lax.optimization_barrier((activations, cw, left, *packed))
    got = [shift(p, "x", s) for s, p in zip((1, 2, 3), packed)]
    gathered = lax.all_gather(act, ("x", "core"), axis=0, tiled=True)
    cw = reduce_scatter(cw.reshape(rank, 2, tok).transpose(1, 0, 2), "core")

    cw3 = jnp.concatenate(split3(cw), 0)
    left = left + fold3(mm(cw3, activations, 1, 0))
    tiles = left.reshape(rank // 8, 8, d // 128, 128).transpose(0, 2, 1, 3).reshape(-1, 8, 128)
    n_tiles = tiles.shape[0]
    part = reduce_scatter(tiles.reshape(2, n_tiles // 2, 8, 128), "core")

    part = reduce_scatter(part.reshape(4, n_tiles // 8, 8, 128), "z")
    part, *got = lax.optimization_barrier((part, *got))

    (cot_own,) = copy_call(
        functools.partial(unpack_plan, tok), 8, [cotangent, cot_other] + got, [like(8, tok, cols)], at, "unpack"
    )
    part, cot_own = lax.optimization_barrier((part, cot_own))
    c_low, c_high = shift(cot_own, "z", 1), shift(cot_own, "z", -1)
    part = reduce_scatter(part.reshape(4, n_tiles // 32, 8, 128), "y")
    part = all_sum(part, "x")
    part, c_low, c_high, w_all = lax.optimization_barrier((part, c_low, c_high, w_all))
    w_other = shift(w_all, "core", 1)
    half = tok // 2
    c_far = [shift(c_low[:, :half], "z", 1), shift(c_high[:, half:], "z", -1)]
    part = all_blocks(part, ("z", "y")).reshape(-1, 8, 128)
    grads = input_call([cot_own, c_low, c_high, *c_far], w_all, w_other, at, 2)
    part, *grads = lax.optimization_barrier((part, *grads))
    back = [grads[0], shift(grads[1], "z", -1), shift(grads[2], "z", 1), shift(grads[3], "z", 2)]
    part = both_cores(part)
    left = part.reshape(rank // 8, d // 128, 8, 128).transpose(0, 2, 1, 3).reshape(rank, d)

    left3 = jnp.concatenate(split3(left), 0)
    right = fold3(mm(left3, activations, 1, 1)) * scale
    right = both_cores(right)
    pieces = [right] + [shift(right, "x", s) for s in (1, 2, 3)]
    right = [sum(jnp.where((ix - s) % 4 == k, p, 0.0) for s, p in enumerate(pieces)) for k in range(4)]
    right = jnp.concatenate([r[c] for r in right for c in (0, 1)], 1)
    right3 = jnp.concatenate(split3(right), 0)
    sums = fold3(mm(right3, cotangent, 1, 0)) + fold3(mm(left3, residual, 1, 0))
    left, right = lax.optimization_barrier((left, right))
    inverse = inverse_of_factor(left)
    sums = all_sum(sums, "y")
    sums, inverse, *back = lax.optimization_barrier((sums, inverse, *back))
    (input_grads,) = copy_call(functools.partial(place_plan, quarter), 4, back, [like(tok, d)], at, "place")
    sums = all_sum(sums, "z")
    factor = jnp.dot(inverse, sums, precision=lax.Precision.HIGHEST) * (1.0 / 16)
    new_residual = residual_call(scale, gathered, cotangent, residual, left, inverse, factor, 1536 if d % 1536 == 0 else 1024)
    return factor.T, new_residual[None], input_grads


def solution(mesh):
    fine = Mesh(mesh.devices.reshape(4, 4, 4, 2), ("y", "z", "x", "core"))
    dp, tensor = ("y", "z"), ("x", "core")
    in_specs = (
        P(dp + tensor, None),
        P(dp, tensor),
        P(None, tensor),
        P(dp, None, tensor),
        P(tensor, None),
    )
    out_specs = (P(tensor, None), P(dp, None, tensor), P(dp + tensor, None))
    return jax.shard_map(per_device, mesh=fine, in_specs=in_specs, out_specs=out_specs, check_vma=False)
```

```python
import functools
import math

import jax
import jax.numpy as jnp
from jax import lax
from jax.experimental import pallas as pl
from jax.experimental.pallas import tpu as pltpu
from jax.sharding import Mesh, PartitionSpec as P

BF16, F32 = jnp.bfloat16, jnp.float32
SIZE = {"y": 4, "z": 4, "x": 4, "core": 2}
VMEM_LIMIT = 56 * 1024 * 1024


def shift(value, axis, step):
    n = SIZE[axis]
    return lax.ppermute(value, axis, [(i, (i + step) % n) for i in range(n)])


def split3(value):
    high = lax.reduce_precision(value, 8, 7)
    rest = value - high
    mid = lax.reduce_precision(rest, 8, 7)
    return high.astype(BF16), mid.astype(BF16), (rest - mid).astype(BF16)


def parts3(value):
    high = value.astype(BF16)
    rest = value - high.astype(F32)
    mid = rest.astype(BF16)
    return high, mid, (rest - mid.astype(F32)).astype(BF16)


def fold3(value):
    rows = value.shape[0] // 3
    return value[:rows] + value[rows : 2 * rows] + value[2 * rows :]


def mm(a, b, ca, cb):
    return lax.dot_general(a, b, (((ca,), (cb,)), ((), ())), preferred_element_type=F32)


def block(value, index):
    return lax.dynamic_index_in_dim(value, index, 0, False)


def reduce_scatter(value, axis):
    n, me = SIZE[axis], lax.axis_index(axis)
    parts = [shift(block(value, (me + s) % n), axis, s) for s in range(1, n)]
    total = block(value, me)
    for part in parts:
        total = total + part
    return total


def all_sum(value, axis):
    parts = [shift(value, axis, s) for s in range(1, SIZE[axis])]
    for part in parts:
        value = value + part
    return value


def all_blocks(value, axis):
    n = math.prod(SIZE[a] for a in axis)
    return lax.all_to_all(jnp.broadcast_to(value[None], (n,) + value.shape), axis, 0, 0)


def both_cores(value):
    other = shift(value, "core", 1)
    first = lax.axis_index("core") == 0
    return jnp.stack([jnp.where(first, value, other), jnp.where(first, other, value)])


def inverse_kernel(left_ref, out_ref):
    n = out_ref.shape[0]
    left3 = jnp.concatenate(parts3(left_ref[...]), 0)
    grams = mm(left3, left3, 1, 1)
    gram = fold3(grams[:, :n] + grams[:, n : 2 * n] + grams[:, 2 * n :])
    row = lax.broadcasted_iota(jnp.int32, (n, 2 * n), 0)
    col = lax.broadcasted_iota(jnp.int32, (n, 2 * n), 1)
    eye = jnp.where(row + n == col, 1.0, 0.0).astype(F32)
    work = jnp.concatenate([gram, jnp.zeros((n, n), F32)], axis=1) + eye
    for k in range(n - 1):
        pivot_row = work[k : k + 1, :]
        pivot = jnp.sum(jnp.where(col[:1] == k, pivot_row, 0.0), axis=1, keepdims=True)
        column = jnp.sum(jnp.where(col == k, work, 0.0), axis=1, keepdims=True)
        work = work - jnp.where(row[:, :1] > k, column / pivot, 0.0) * pivot_row
    pivots = jnp.sum(jnp.where(row == col, work, 0.0), axis=1, keepdims=True)
    root = lax.rsqrt(pivots)
    root = root * (1.5 - 0.5 * pivots * root * root)
    out_ref[...] = work[:, n:] * root


def inverse_of_factor(left):
    rank = left.shape[0]
    return pl.pallas_call(
        inverse_kernel,
        out_shape=jax.ShapeDtypeStruct((rank, rank), F32),
        name="inverse_of_factor",
    )(left)


def residual_kernel(scale, sizes, act_ref, cot_ref, residual_ref, left_ref, inverse_ref, factor_ref, out_ref, acts, olds, news, sems):
    f_h, f_m, f_l = parts3(factor_ref[...])
    factor6 = jnp.concatenate([f_h, f_h, f_h, f_m, f_m, f_l], 0)
    starts = [sum(sizes[:i]) for i in range(len(sizes))]

    def loads(i):
        slot, span = i % 2, pl.ds(starts[i], sizes[i])
        return (
            pltpu.make_async_copy(act_ref.at[:, span], acts.at[slot, :, pl.ds(0, sizes[i])], sems.at[0, slot]),
            pltpu.make_async_copy(residual_ref.at[span], olds.at[slot, pl.ds(0, sizes[i])], sems.at[1, slot]),
        )

    def store(i):
        slot = i % 2
        return pltpu.make_async_copy(news.at[slot, pl.ds(0, sizes[i])], out_ref.at[pl.ds(starts[i], sizes[i])], sems.at[2, slot])

    for i in (0, 1):
        for copy in loads(i):
            copy.start()
    for i, size in enumerate(sizes):
        slot = i % 2
        basis = lax.dot_general(
            inverse_ref[...],
            left_ref[:, starts[i] : starts[i] + size],
            (((1,), (0,)), ((), ())),
            precision=lax.Precision.HIGHEST,
            preferred_element_type=F32,
        )
        b_h, b_m, b_l = parts3(basis)
        basis6 = jnp.concatenate([b_h, b_m, b_l, b_h, b_m, b_h], 0)
        for copy in loads(i):
            copy.wait()
        if i >= 2:
            store(i - 2).wait()
        total = mm(acts[slot, :, :size], cot_ref[...], 0, 0) * scale + olds[slot, :size].astype(F32)
        news[slot, :size] = (total - mm(basis6, factor6, 0, 0)).astype(BF16)
        store(i).start()
        if i + 2 < len(sizes):
            for copy in loads(i + 2):
                copy.start()
    for i in range(len(sizes))[-2:]:
        store(i).wait()


def residual_call(scale, act, cot, residual, left, inverse, factor, sizes):
    k, d = act.shape
    cols, rank = cot.shape[1], left.shape[0]
    held, most = pl.BlockSpec(memory_space=pl.ANY), max(sizes)
    whole = pl.BlockSpec(memory_space=pltpu.VMEM)
    return pl.pallas_call(
        functools.partial(residual_kernel, scale, tuple(sizes)),
        out_shape=jax.ShapeDtypeStruct((d, cols), BF16),
        in_specs=[held, whole, held, whole, whole, whole],
        out_specs=held,
        scratch_shapes=[
            pltpu.VMEM((2, k, most), BF16),
            pltpu.VMEM((2, most, cols), BF16),
            pltpu.VMEM((2, most, cols), BF16),
            pltpu.SemaphoreType.DMA((3, 2)),
        ],
        compiler_params=pltpu.CompilerParams(vmem_limit_bytes=52 * 1024 * 1024),
        cost_estimate=pl.CostEstimate(
            flops=2 * d * cols * (k + 6 * rank), bytes_accessed=2 * d * k + 4 * d * cols + 4 * d * rank, transcendentals=0
        ),
        name="new_residual",
    )(act, cot, residual, left, inverse, factor)


def input_kernel(n_cot, at_ref, *refs):
    cots, weights, outs = refs[:n_cot], refs[n_cot : n_cot + 2], refs[n_cot + 2 :]
    blocks, chips = weights[0].shape[:2]
    tok, width = outs[0].shape
    total = jnp.zeros((tok * len(outs), width), F32)
    for s in range(chips):
        tokens = jnp.concatenate([jnp.concatenate([c[2 * s], c[2 * s + 1]], 1) for c in cots], 0)
        rows = [jnp.concatenate([w[b, at_ref[4 + s]] for w in weights], 1) for b in range(blocks)]
        total = total + mm(tokens, jnp.concatenate(rows, 0), 1, 1)
    for i, out in enumerate(outs):
        out[...] = total[i * tok : (i + 1) * tok].astype(BF16)


def input_call(cots, weight, other, at, blocks):
    n, chips, rows, cols = weight.shape
    _, tok, _ = cots[0].shape
    tokens = 4 * tok
    return pl.pallas_call(
        functools.partial(input_kernel, len(cots)),
        out_shape=[jax.ShapeDtypeStruct((tok, n * rows), BF16)] * 4,
        grid_spec=pltpu.PrefetchScalarGridSpec(
            num_scalar_prefetch=1,
            grid=(n // blocks,),
            in_specs=[pl.BlockSpec(c.shape, lambda i, q: (0, 0, 0)) for c in cots]
            + [pl.BlockSpec((blocks, chips, rows, cols), lambda i, q: (i, 0, 0, 0))] * 2,
            out_specs=[pl.BlockSpec((tok, blocks * rows), lambda i, q: (0, i))] * 4,
        ),
        compiler_params=pltpu.CompilerParams(vmem_limit_bytes=VMEM_LIMIT),
        cost_estimate=pl.CostEstimate(
            flops=2 * tokens * n * rows * cols * 8, bytes_accessed=16 * cols * (tokens + n * rows), transcendentals=0
        ),
        name="input_grads",
    )(at, *cots, weight, other)


def copy_kernel(n_in, n_out, plan, at_ref, *refs):
    ins, outs, sems = refs[:n_in], refs[n_in : n_in + n_out], refs[n_in + n_out]
    copies = [pltpu.make_async_copy(*pair, sems.at[i]) for i, pair in enumerate(plan(at_ref, ins, outs))]
    for copy in copies:
        copy.start()
    for copy in copies:
        copy.wait()


def copy_call(plan, n_copies, ins, outs, at, name, vmem=16 * 1024 * 1024):
    any_spec = pl.BlockSpec(memory_space=pltpu.HBM)
    moved = sum(2 * math.prod(o.shape) * o.dtype.itemsize for o in outs)
    return pl.pallas_call(
        functools.partial(copy_kernel, len(ins), len(outs), plan),
        out_shape=outs,
        grid_spec=pltpu.PrefetchScalarGridSpec(
            num_scalar_prefetch=1,
            grid=(1,),
            in_specs=[any_spec] * len(ins),
            out_specs=[pl.BlockSpec(o.shape, lambda i, a, n=len(o.shape): (0,) * n) for o in outs],
            scratch_shapes=[pltpu.SemaphoreType.DMA((n_copies,))],
        ),
        compiler_params=pltpu.CompilerParams(vmem_limit_bytes=vmem),
        cost_estimate=pl.CostEstimate(flops=0, bytes_accessed=moved, transcendentals=0),
        name=name,
    )(at, *ins)


def part_of(ref, index, size):
    return ref.at[pl.ds(pl.multiple_of(index * size, size), size)]


def pack_plan(tok, at, ins, outs):
    return [
        (part_of(cot, at[s], tok), out.at[pl.ds(i * tok, tok)]) for s, out in zip((1, 2, 3), outs) for i, cot in enumerate(ins)
    ]


def unpack_plan(tok, at, ins, outs):
    cot, other, *got = ins
    pairs = [(part_of(cot, at[0], tok), outs[0].at[0]), (part_of(other, at[0], tok), outs[0].at[1])]
    return pairs + [(g.at[pl.ds(i * tok, tok)], outs[0].at[2 * s + 2 + i]) for s, g in enumerate(got) for i in (0, 1)]


def place_plan(width, at, ins, outs):
    return [(r, outs[0].at[:, pl.ds(pl.multiple_of(at[8 + i] * width, width), width)]) for i, r in enumerate(ins)]


def per_device(activations, cotangent, weight, residual, warm_factor):
    iy, iz, ix, ic = (lax.axis_index(a) for a in ("y", "z", "x", "core"))
    tok, d = activations.shape
    tok_dev, cols = cotangent.shape
    rank = warm_factor.shape[1]
    residual = residual[0]
    scale = tok_dev ** (-0.5)
    quarter = d // 4
    sub = quarter // 4

    like = lambda *shape: jax.ShapeDtypeStruct(shape, BF16)
    w_send = lax.dynamic_slice_in_dim(weight, iz * quarter + iy * sub, sub, 0)
    w_all = lax.all_gather(w_send, ("y", "x")).reshape(4, 4, sub, cols)

    cot_other = shift(cotangent, "core", 1)
    at = [((ix + s) % 4) * 2 + ic for s in range(4)] + [(ix - s) % 4 for s in range(4)]
    at = jnp.stack(at + [(iz + s) % 4 for s in (0, 1, -1, 2)]).astype(jnp.int32)
    packed = copy_call(functools.partial(pack_plan, tok), 6, [cotangent, cot_other], [like(2 * tok, cols)] * 3, at, "pack", VMEM_LIMIT)

    warm3 = jnp.concatenate(split3(warm_factor.T), 0)
    cw = fold3(mm(warm3, cotangent, 1, 1)) * scale
    cw = reduce_scatter(cw.reshape(rank, 4, 2 * tok).transpose(1, 0, 2), "x")
    left = fold3(mm(warm3, residual, 1, 1))
    act, cw, left, *packed = lax.optimization_barrier((activations, cw, left, *packed))
    got = [shift(p, "x", s) for s, p in zip((1, 2, 3), packed)]
    gathered = lax.all_gather(act, ("x", "core"), axis=0, tiled=True)
    cw = reduce_scatter(cw.reshape(rank, 2, tok).transpose(1, 0, 2), "core")

    cw3 = jnp.concatenate(split3(cw), 0)
    left = left + fold3(mm(cw3, activations, 1, 0))
    tiles = left.reshape(rank // 8, 8, d // 128, 128).transpose(0, 2, 1, 3).reshape(-1, 8, 128)
    n_tiles = tiles.shape[0]
    part = reduce_scatter(tiles.reshape(2, n_tiles // 2, 8, 128), "core")

    part = reduce_scatter(part.reshape(4, n_tiles // 8, 8, 128), "z")
    part, *got = lax.optimization_barrier((part, *got))

    (cot_own,) = copy_call(
        functools.partial(unpack_plan, tok), 8, [cotangent, cot_other] + got, [like(8, tok, cols)], at, "unpack"
    )
    part, cot_own = lax.optimization_barrier((part, cot_own))
    c_low, c_high = shift(cot_own, "z", 1), shift(cot_own, "z", -1)
    part = reduce_scatter(part.reshape(4, n_tiles // 32, 8, 128), "y")
    part = all_sum(part, "x")
    part, c_low, c_high, w_all = lax.optimization_barrier((part, c_low, c_high, w_all))
    w_other = shift(w_all, "core", 1)
    half = tok // 2
    c_far = [shift(c_low[:, :half], "z", 1), shift(c_high[:, half:], "z", -1)]
    part = all_blocks(part, ("z", "y")).reshape(-1, 8, 128)
    grads = input_call([cot_own, c_low, c_high, *c_far], w_all, w_other, at, 2)
    part, *grads = lax.optimization_barrier((part, *grads))
    back = [grads[0], shift(grads[1], "z", -1), shift(grads[2], "z", 1), shift(grads[3], "z", 2)]
    part = both_cores(part)
    left = part.reshape(rank // 8, d // 128, 8, 128).transpose(0, 2, 1, 3).reshape(rank, d)

    left3 = jnp.concatenate(split3(left), 0)
    right = fold3(mm(left3, activations, 1, 1)) * scale
    right = both_cores(right)
    pieces = [right] + [shift(right, "x", s) for s in (1, 2, 3)]
    right = [sum(jnp.where((ix - s) % 4 == k, p, 0.0) for s, p in enumerate(pieces)) for k in range(4)]
    right = jnp.concatenate([r[c] for r in right for c in (0, 1)], 1)
    right3 = jnp.concatenate(split3(right), 0)
    sums = fold3(mm(right3, cotangent, 1, 0)) + fold3(mm(left3, residual, 1, 0))
    left, right = lax.optimization_barrier((left, right))
    inverse = inverse_of_factor(left)
    sums = all_sum(sums, "y")
    sums, inverse, *back = lax.optimization_barrier((sums, inverse, *back))
    (input_grads,) = copy_call(functools.partial(place_plan, quarter), 4, back, [like(tok, d)], at, "place")
    sums = all_sum(sums, "z")
    factor = jnp.dot(inverse, sums, precision=lax.Precision.HIGHEST) * (1.0 / 16)
    sizes = [d // 12 * w for w in (1, 2, 3, 3, 2, 1)] if d % 1536 == 0 else [d // 2] * 2
    new_residual = residual_call(scale, gathered, cotangent, residual, left, inverse, factor, sizes)
    return factor.T, new_residual[None], input_grads


def solution(mesh):
    fine = Mesh(mesh.devices.reshape(4, 4, 4, 2), ("y", "z", "x", "core"))
    dp, tensor = ("y", "z"), ("x", "core")
    in_specs = (
        P(dp + tensor, None),
        P(dp, tensor),
        P(None, tensor),
        P(dp, None, tensor),
        P(tensor, None),
    )
    out_specs = (P(tensor, None), P(dp, None, tensor), P(dp + tensor, None))
    return jax.shard_map(per_device, mesh=fine, in_specs=in_specs, out_specs=out_specs, check_vma=False)
```

```python
import functools
import math

import jax
import jax.numpy as jnp
from jax import lax
from jax.experimental import pallas as pl
from jax.experimental.pallas import tpu as pltpu
from jax.sharding import Mesh, PartitionSpec as P

BF16, F32 = jnp.bfloat16, jnp.float32
SIZE = {"y": 4, "z": 4, "x": 4, "core": 2}
VMEM_LIMIT = 56 * 1024 * 1024


def shift(value, axis, step):
    n = SIZE[axis]
    return lax.ppermute(value, axis, [(i, (i + step) % n) for i in range(n)])


def split3(value):
    high = lax.reduce_precision(value, 8, 7)
    rest = value - high
    mid = lax.reduce_precision(rest, 8, 7)
    return high.astype(BF16), mid.astype(BF16), (rest - mid).astype(BF16)


def parts3(value):
    high = value.astype(BF16)
    rest = value - high.astype(F32)
    mid = rest.astype(BF16)
    return high, mid, (rest - mid.astype(F32)).astype(BF16)


def fold3(value):
    rows = value.shape[0] // 3
    return value[:rows] + value[rows : 2 * rows] + value[2 * rows :]


def mm(a, b, ca, cb):
    return lax.dot_general(a, b, (((ca,), (cb,)), ((), ())), preferred_element_type=F32)


def block(value, index):
    return lax.dynamic_index_in_dim(value, index, 0, False)


def reduce_scatter(value, axis):
    n, me = SIZE[axis], lax.axis_index(axis)
    parts = [shift(block(value, (me + s) % n), axis, s) for s in range(1, n)]
    total = block(value, me)
    for part in parts:
        total = total + part
    return total


def all_sum(value, axis):
    parts = [shift(value, axis, s) for s in range(1, SIZE[axis])]
    for part in parts:
        value = value + part
    return value


def all_blocks(value, axis):
    n = math.prod(SIZE[a] for a in axis)
    return lax.all_to_all(jnp.broadcast_to(value[None], (n,) + value.shape), axis, 0, 0)


def both_cores(value):
    other = shift(value, "core", 1)
    first = lax.axis_index("core") == 0
    return jnp.stack([jnp.where(first, value, other), jnp.where(first, other, value)])


def inverse_kernel(left_ref, out_ref):
    n = out_ref.shape[0]
    left3 = jnp.concatenate(parts3(left_ref[...]), 0)
    grams = mm(left3, left3, 1, 1)
    gram = fold3(grams[:, :n] + grams[:, n : 2 * n] + grams[:, 2 * n :])
    row = lax.broadcasted_iota(jnp.int32, (n, 2 * n), 0)
    col = lax.broadcasted_iota(jnp.int32, (n, 2 * n), 1)
    eye = jnp.where(row + n == col, 1.0, 0.0).astype(F32)
    work = jnp.concatenate([gram, jnp.zeros((n, n), F32)], axis=1) + eye
    for k in range(n - 1):
        pivot_row = work[k : k + 1, :]
        pivot = jnp.sum(jnp.where(col[:1] == k, pivot_row, 0.0), axis=1, keepdims=True)
        column = jnp.sum(jnp.where(col == k, work, 0.0), axis=1, keepdims=True)
        work = work - jnp.where(row[:, :1] > k, column / pivot, 0.0) * pivot_row
    pivots = jnp.sum(jnp.where(row == col, work, 0.0), axis=1, keepdims=True)
    root = lax.rsqrt(pivots)
    root = root * (1.5 - 0.5 * pivots * root * root)
    out_ref[...] = work[:, n:] * root


def inverse_of_factor(left):
    rank = left.shape[0]
    return pl.pallas_call(
        inverse_kernel,
        out_shape=jax.ShapeDtypeStruct((rank, rank), F32),
        name="inverse_of_factor",
    )(left)


def residual_kernel(scale, sizes, act_ref, cot_ref, residual_ref, left_ref, inverse_ref, factor_ref, out_ref, acts, olds, news, sems):
    f_h, f_m, f_l = parts3(factor_ref[...])
    factor6 = jnp.concatenate([f_h, f_h, f_h, f_m, f_m, f_l], 0)
    starts = [sum(sizes[:i]) for i in range(len(sizes))]

    def loads(i):
        slot, span = i % 2, pl.ds(starts[i], sizes[i])
        return (
            pltpu.make_async_copy(act_ref.at[:, span], acts.at[slot, :, pl.ds(0, sizes[i])], sems.at[0, slot]),
            pltpu.make_async_copy(residual_ref.at[span], olds.at[slot, pl.ds(0, sizes[i])], sems.at[1, slot]),
        )

    def store(i):
        slot = i % 2
        return pltpu.make_async_copy(news.at[slot, pl.ds(0, sizes[i])], out_ref.at[pl.ds(starts[i], sizes[i])], sems.at[2, slot])

    for i in (0, 1):
        for copy in loads(i):
            copy.start()
    cot = cot_ref[...].T
    for i, size in enumerate(sizes):
        slot = i % 2
        basis = lax.dot_general(
            inverse_ref[...],
            left_ref[:, starts[i] : starts[i] + size],
            (((1,), (0,)), ((), ())),
            precision=lax.Precision.HIGHEST,
            preferred_element_type=F32,
        )
        b_h, b_m, b_l = parts3(basis)
        basis6 = jnp.concatenate([b_h, b_m, b_l, b_h, b_m, b_h], 0)
        for copy in loads(i):
            copy.wait()
        if i >= 2:
            store(i - 2).wait()
        total = mm(cot, acts[slot, :, :size], 1, 0) * scale - mm(factor6, basis6, 0, 0)
        news[slot, :size] = (total.T + olds[slot, :size].astype(F32)).astype(BF16)
        store(i).start()
        if i + 2 < len(sizes):
            for copy in loads(i + 2):
                copy.start()
    for i in range(len(sizes))[-2:]:
        store(i).wait()


def residual_call(scale, act, cot, residual, left, inverse, factor, sizes):
    k, d = act.shape
    cols, rank = cot.shape[1], left.shape[0]
    held, most = pl.BlockSpec(memory_space=pl.ANY), max(sizes)
    whole = pl.BlockSpec(memory_space=pltpu.VMEM)
    return pl.pallas_call(
        functools.partial(residual_kernel, scale, tuple(sizes)),
        out_shape=jax.ShapeDtypeStruct((d, cols), BF16),
        in_specs=[held, whole, held, whole, whole, whole],
        out_specs=held,
        scratch_shapes=[
            pltpu.VMEM((2, k, most), BF16),
            pltpu.VMEM((2, most, cols), BF16),
            pltpu.VMEM((2, most, cols), BF16),
            pltpu.SemaphoreType.DMA((3, 2)),
        ],
        compiler_params=pltpu.CompilerParams(vmem_limit_bytes=52 * 1024 * 1024),
        cost_estimate=pl.CostEstimate(
            flops=2 * d * cols * (k + 6 * rank), bytes_accessed=2 * d * k + 4 * d * cols + 4 * d * rank, transcendentals=0
        ),
        name="new_residual",
    )(act, cot, residual, left, inverse, factor)


def input_kernel(n_cot, at_ref, *refs):
    cots, weights, outs = refs[:n_cot], refs[n_cot : n_cot + 2], refs[n_cot + 2 :]
    blocks, chips = weights[0].shape[:2]
    tok, width = outs[0].shape
    total = jnp.zeros((tok * len(outs), width), F32)
    for s in range(chips):
        tokens = jnp.concatenate([jnp.concatenate([c[2 * s], c[2 * s + 1]], 1) for c in cots], 0)
        rows = [jnp.concatenate([w[b, at_ref[4 + s]] for w in weights], 1) for b in range(blocks)]
        total = total + mm(tokens, jnp.concatenate(rows, 0), 1, 1)
    for i, out in enumerate(outs):
        out[...] = total[i * tok : (i + 1) * tok].astype(BF16)


def input_call(cots, weight, other, at, blocks):
    n, chips, rows, cols = weight.shape
    _, tok, _ = cots[0].shape
    tokens = 4 * tok
    return pl.pallas_call(
        functools.partial(input_kernel, len(cots)),
        out_shape=[jax.ShapeDtypeStruct((tok, n * rows), BF16)] * 4,
        grid_spec=pltpu.PrefetchScalarGridSpec(
            num_scalar_prefetch=1,
            grid=(n // blocks,),
            in_specs=[pl.BlockSpec(c.shape, lambda i, q: (0, 0, 0)) for c in cots]
            + [pl.BlockSpec((blocks, chips, rows, cols), lambda i, q: (i, 0, 0, 0))] * 2,
            out_specs=[pl.BlockSpec((tok, blocks * rows), lambda i, q: (0, i))] * 4,
        ),
        compiler_params=pltpu.CompilerParams(vmem_limit_bytes=VMEM_LIMIT),
        cost_estimate=pl.CostEstimate(
            flops=2 * tokens * n * rows * cols * 8, bytes_accessed=16 * cols * (tokens + n * rows), transcendentals=0
        ),
        name="input_grads",
    )(at, *cots, weight, other)


def copy_kernel(n_in, n_out, plan, at_ref, *refs):
    ins, outs, sems = refs[:n_in], refs[n_in : n_in + n_out], refs[n_in + n_out]
    copies = [pltpu.make_async_copy(*pair, sems.at[i]) for i, pair in enumerate(plan(at_ref, ins, outs))]
    for copy in copies:
        copy.start()
    for copy in copies:
        copy.wait()


def copy_call(plan, n_copies, ins, outs, at, name, vmem=16 * 1024 * 1024):
    any_spec = pl.BlockSpec(memory_space=pltpu.HBM)
    moved = sum(2 * math.prod(o.shape) * o.dtype.itemsize for o in outs)
    return pl.pallas_call(
        functools.partial(copy_kernel, len(ins), len(outs), plan),
        out_shape=outs,
        grid_spec=pltpu.PrefetchScalarGridSpec(
            num_scalar_prefetch=1,
            grid=(1,),
            in_specs=[any_spec] * len(ins),
            out_specs=[pl.BlockSpec(o.shape, lambda i, a, n=len(o.shape): (0,) * n) for o in outs],
            scratch_shapes=[pltpu.SemaphoreType.DMA((n_copies,))],
        ),
        compiler_params=pltpu.CompilerParams(vmem_limit_bytes=vmem),
        cost_estimate=pl.CostEstimate(flops=0, bytes_accessed=moved, transcendentals=0),
        name=name,
    )(at, *ins)


def part_of(ref, index, size):
    return ref.at[pl.ds(pl.multiple_of(index * size, size), size)]


def pack_plan(tok, at, ins, outs):
    return [
        (part_of(cot, at[s], tok), out.at[pl.ds(i * tok, tok)]) for s, out in zip((1, 2, 3), outs) for i, cot in enumerate(ins)
    ]


def unpack_plan(tok, at, ins, outs):
    cot, other, *got = ins
    pairs = [(part_of(cot, at[0], tok), outs[0].at[0]), (part_of(other, at[0], tok), outs[0].at[1])]
    return pairs + [(g.at[pl.ds(i * tok, tok)], outs[0].at[2 * s + 2 + i]) for s, g in enumerate(got) for i in (0, 1)]


def place_plan(width, at, ins, outs):
    return [(r, outs[0].at[:, pl.ds(pl.multiple_of(at[8 + i] * width, width), width)]) for i, r in enumerate(ins)]


def per_device(activations, cotangent, weight, residual, warm_factor):
    iy, iz, ix, ic = (lax.axis_index(a) for a in ("y", "z", "x", "core"))
    tok, d = activations.shape
    tok_dev, cols = cotangent.shape
    rank = warm_factor.shape[1]
    residual = residual[0]
    scale = tok_dev ** (-0.5)
    quarter = d // 4
    sub = quarter // 4

    like = lambda *shape: jax.ShapeDtypeStruct(shape, BF16)
    w_send = lax.dynamic_slice_in_dim(weight, iz * quarter + iy * sub, sub, 0)
    w_all = lax.all_gather(w_send, ("y", "x")).reshape(4, 4, sub, cols)

    cot_other = shift(cotangent, "core", 1)
    at = [((ix + s) % 4) * 2 + ic for s in range(4)] + [(ix - s) % 4 for s in range(4)]
    at = jnp.stack(at + [(iz + s) % 4 for s in (0, 1, -1, 2)]).astype(jnp.int32)
    packed = copy_call(functools.partial(pack_plan, tok), 6, [cotangent, cot_other], [like(2 * tok, cols)] * 3, at, "pack", VMEM_LIMIT)

    warm3 = jnp.concatenate(split3(warm_factor.T), 0)
    cw = fold3(mm(warm3, cotangent, 1, 1)) * scale
    cw = reduce_scatter(cw.reshape(rank, 4, 2 * tok).transpose(1, 0, 2), "x")
    left = fold3(mm(warm3, residual, 1, 1))
    act, cw, left, *packed = lax.optimization_barrier((activations, cw, left, *packed))
    got = [shift(p, "x", s) for s, p in zip((1, 2, 3), packed)]
    gathered = lax.all_gather(act, ("x", "core"), axis=0, tiled=True)
    cw = reduce_scatter(cw.reshape(rank, 2, tok).transpose(1, 0, 2), "core")

    cw3 = jnp.concatenate(split3(cw), 0)
    left = left + fold3(mm(cw3, activations, 1, 0))
    tiles = left.reshape(rank // 8, 8, d // 128, 128).transpose(0, 2, 1, 3).reshape(-1, 8, 128)
    n_tiles = tiles.shape[0]
    part = reduce_scatter(tiles.reshape(2, n_tiles // 2, 8, 128), "core")

    part = reduce_scatter(part.reshape(4, n_tiles // 8, 8, 128), "z")
    part, *got = lax.optimization_barrier((part, *got))

    (cot_own,) = copy_call(
        functools.partial(unpack_plan, tok), 8, [cotangent, cot_other] + got, [like(8, tok, cols)], at, "unpack"
    )
    part, cot_own = lax.optimization_barrier((part, cot_own))
    c_low, c_high = shift(cot_own, "z", 1), shift(cot_own, "z", -1)
    part = reduce_scatter(part.reshape(4, n_tiles // 32, 8, 128), "y")
    part = all_sum(part, "x")
    part, c_low, c_high, w_all = lax.optimization_barrier((part, c_low, c_high, w_all))
    w_other = shift(w_all, "core", 1)
    half = tok // 2
    c_far = [shift(c_low[:, :half], "z", 1), shift(c_high[:, half:], "z", -1)]
    part = all_blocks(part, ("z", "y")).reshape(-1, 8, 128)
    grads = input_call([cot_own, c_low, c_high, *c_far], w_all, w_other, at, 2)
    part, *grads = lax.optimization_barrier((part, *grads))
    back = [grads[0], shift(grads[1], "z", -1), shift(grads[2], "z", 1), shift(grads[3], "z", 2)]
    part = both_cores(part)
    left = part.reshape(rank // 8, d // 128, 8, 128).transpose(0, 2, 1, 3).reshape(rank, d)

    left3 = jnp.concatenate(split3(left), 0)
    right = fold3(mm(left3, activations, 1, 1)) * scale
    right = both_cores(right)
    pieces = [right] + [shift(right, "x", s) for s in (1, 2, 3)]
    right = [sum(jnp.where((ix - s) % 4 == k, p, 0.0) for s, p in enumerate(pieces)) for k in range(4)]
    right = jnp.concatenate([r[c] for r in right for c in (0, 1)], 1)
    right3 = jnp.concatenate(split3(right), 0)
    sums = fold3(mm(right3, cotangent, 1, 0)) + fold3(mm(left3, residual, 1, 0))
    left, right = lax.optimization_barrier((left, right))
    inverse = inverse_of_factor(left)
    sums = all_sum(sums, "y")
    sums, inverse, *back = lax.optimization_barrier((sums, inverse, *back))
    (input_grads,) = copy_call(functools.partial(place_plan, quarter), 4, back, [like(tok, d)], at, "place")
    sums = all_sum(sums, "z")
    factor = jnp.dot(inverse, sums, precision=lax.Precision.HIGHEST) * (1.0 / 16)
    sizes = [d // 12 * w for w in (1, 2, 3, 3, 2, 1)] if d % 1536 == 0 else [d // 2] * 2
    new_residual = residual_call(scale, gathered, cotangent, residual, left, inverse, factor, sizes)
    return factor.T, new_residual[None], input_grads


def solution(mesh):
    fine = Mesh(mesh.devices.reshape(4, 4, 4, 2), ("y", "z", "x", "core"))
    dp, tensor = ("y", "z"), ("x", "core")
    in_specs = (
        P(dp + tensor, None),
        P(dp, tensor),
        P(None, tensor),
        P(dp, None, tensor),
        P(tensor, None),
    )
    out_specs = (P(tensor, None), P(dp, None, tensor), P(dp + tensor, None))
    return jax.shard_map(per_device, mesh=fine, in_specs=in_specs, out_specs=out_specs, check_vma=False)
```

```python
import functools
import math

import jax
import jax.numpy as jnp
from jax import lax
from jax.experimental import pallas as pl
from jax.experimental.pallas import tpu as pltpu
from jax.sharding import Mesh, PartitionSpec as P

BF16, F32 = jnp.bfloat16, jnp.float32
SIZE = {"y": 4, "z": 4, "x": 4, "core": 2}
VMEM_LIMIT = 56 * 1024 * 1024


def shift(value, axis, step):
    n = SIZE[axis]
    return lax.ppermute(value, axis, [(i, (i + step) % n) for i in range(n)])


def split3(value):
    high = lax.reduce_precision(value, 8, 7)
    rest = value - high
    mid = lax.reduce_precision(rest, 8, 7)
    return high.astype(BF16), mid.astype(BF16), (rest - mid).astype(BF16)


def parts3(value):
    high = value.astype(BF16)
    rest = value - high.astype(F32)
    mid = rest.astype(BF16)
    return high, mid, (rest - mid.astype(F32)).astype(BF16)


def fold3(value):
    rows = value.shape[0] // 3
    return value[:rows] + value[rows : 2 * rows] + value[2 * rows :]


def mm(a, b, ca, cb):
    return lax.dot_general(a, b, (((ca,), (cb,)), ((), ())), preferred_element_type=F32)


def block(value, index):
    return lax.dynamic_index_in_dim(value, index, 0, False)


def reduce_scatter(value, axis):
    n, me = SIZE[axis], lax.axis_index(axis)
    parts = [shift(block(value, (me + s) % n), axis, s) for s in range(1, n)]
    total = block(value, me)
    for part in parts:
        total = total + part
    return total


def all_sum(value, axis):
    parts = [shift(value, axis, s) for s in range(1, SIZE[axis])]
    for part in parts:
        value = value + part
    return value


def all_blocks(value, axis):
    n = math.prod(SIZE[a] for a in axis)
    return lax.all_to_all(jnp.broadcast_to(value[None], (n,) + value.shape), axis, 0, 0)


def both_cores(value):
    other = shift(value, "core", 1)
    first = lax.axis_index("core") == 0
    return jnp.stack([jnp.where(first, value, other), jnp.where(first, other, value)])


def inverse_kernel(left_ref, out_ref):
    n = out_ref.shape[0]
    left3 = jnp.concatenate(parts3(left_ref[...]), 0)
    grams = mm(left3, left3, 1, 1)
    gram = fold3(grams[:, :n] + grams[:, n : 2 * n] + grams[:, 2 * n :])
    row = lax.broadcasted_iota(jnp.int32, (n, 2 * n), 0)
    col = lax.broadcasted_iota(jnp.int32, (n, 2 * n), 1)
    eye = jnp.where(row + n == col, 1.0, 0.0).astype(F32)
    work = jnp.concatenate([gram, jnp.zeros((n, n), F32)], axis=1) + eye
    for k in range(n - 1):
        pivot_row = work[k : k + 1, :]
        pivot = jnp.sum(jnp.where(col[:1] == k, pivot_row, 0.0), axis=1, keepdims=True)
        column = jnp.sum(jnp.where(col == k, work, 0.0), axis=1, keepdims=True)
        work = work - jnp.where(row[:, :1] > k, column / pivot, 0.0) * pivot_row
    pivots = jnp.sum(jnp.where(row == col, work, 0.0), axis=1, keepdims=True)
    root = lax.rsqrt(pivots)
    root = root * (1.5 - 0.5 * pivots * root * root)
    out_ref[...] = work[:, n:] * root


def inverse_of_factor(left):
    rank = left.shape[0]
    return pl.pallas_call(
        inverse_kernel,
        out_shape=jax.ShapeDtypeStruct((rank, rank), F32),
        name="inverse_of_factor",
    )(left)


def residual_kernel(scale, sizes, act_ref, cot_ref, residual_ref, left_ref, inverse_ref, factor_ref, out_ref, acts, olds, news, sems):
    f_h, f_m, f_l = parts3(factor_ref[...])
    factor6 = jnp.concatenate([f_h, f_h, f_h, f_m, f_m, f_l], 0)
    starts = [sum(sizes[:i]) for i in range(len(sizes))]

    def loads(i):
        slot, span = i % 2, pl.ds(starts[i], sizes[i])
        return (
            pltpu.make_async_copy(act_ref.at[:, span], acts.at[slot, :, pl.ds(0, sizes[i])], sems.at[0, slot]),
            pltpu.make_async_copy(residual_ref.at[span], olds.at[slot, pl.ds(0, sizes[i])], sems.at[1, slot]),
        )

    def store(i):
        slot = i % 2
        return pltpu.make_async_copy(news.at[slot, pl.ds(0, sizes[i])], out_ref.at[pl.ds(starts[i], sizes[i])], sems.at[2, slot])

    for i in (0, 1):
        for copy in loads(i):
            copy.start()
    cot = cot_ref[...].T
    for i, size in enumerate(sizes):
        slot = i % 2
        basis = lax.dot_general(
            inverse_ref[...],
            left_ref[:, starts[i] : starts[i] + size],
            (((1,), (0,)), ((), ())),
            precision=lax.Precision.HIGHEST,
            preferred_element_type=F32,
        )
        b_h, b_m, b_l = parts3(basis)
        basis6 = jnp.concatenate([b_h, b_m, b_l, b_h, b_m, b_h], 0)
        for copy in loads(i):
            copy.wait()
        if i >= 2:
            store(i - 2).wait()
        total = mm(cot, acts[slot, :, :size], 1, 0) * scale - mm(factor6, basis6, 0, 0)
        news[slot, :size] = (total.T + olds[slot, :size].astype(F32)).astype(BF16)
        store(i).start()
        if i + 2 < len(sizes):
            for copy in loads(i + 2):
                copy.start()
    for i in range(len(sizes))[-2:]:
        store(i).wait()


def residual_call(scale, act, cot, residual, left, inverse, factor, sizes):
    k, d = act.shape
    cols, rank = cot.shape[1], left.shape[0]
    held, most = pl.BlockSpec(memory_space=pl.ANY), max(sizes)
    whole = pl.BlockSpec(memory_space=pltpu.VMEM)
    return pl.pallas_call(
        functools.partial(residual_kernel, scale, tuple(sizes)),
        out_shape=jax.ShapeDtypeStruct((d, cols), BF16),
        in_specs=[held, whole, held, whole, whole, whole],
        out_specs=held,
        scratch_shapes=[
            pltpu.VMEM((2, k, most), BF16),
            pltpu.VMEM((2, most, cols), BF16),
            pltpu.VMEM((2, most, cols), BF16),
            pltpu.SemaphoreType.DMA((3, 2)),
        ],
        compiler_params=pltpu.CompilerParams(vmem_limit_bytes=52 * 1024 * 1024),
        cost_estimate=pl.CostEstimate(
            flops=2 * d * cols * (k + 6 * rank), bytes_accessed=2 * d * k + 4 * d * cols + 4 * d * rank, transcendentals=0
        ),
        name="new_residual",
    )(act, cot, residual, left, inverse, factor)


def input_kernel(n_cot, at_ref, *refs):
    cots, weights, outs = refs[:n_cot], refs[n_cot : n_cot + 2], refs[n_cot + 2 :]
    blocks, chips = weights[0].shape[:2]
    tok, width = outs[0].shape
    total = jnp.zeros((tok * len(outs), width), F32)
    for s in range(chips):
        tokens = jnp.concatenate([jnp.concatenate([c[2 * s], c[2 * s + 1]], 1) for c in cots], 0)
        rows = [jnp.concatenate([w[b, at_ref[4 + s]] for w in weights], 1) for b in range(blocks)]
        total = total + mm(tokens, jnp.concatenate(rows, 0), 1, 1)
    for i, out in enumerate(outs):
        out[...] = total[i * tok : (i + 1) * tok].astype(BF16)


def input_call(cots, weight, other, at, blocks):
    n, chips, rows, cols = weight.shape
    _, tok, _ = cots[0].shape
    tokens = 4 * tok
    return pl.pallas_call(
        functools.partial(input_kernel, len(cots)),
        out_shape=[jax.ShapeDtypeStruct((tok, n * rows), BF16)] * 4,
        grid_spec=pltpu.PrefetchScalarGridSpec(
            num_scalar_prefetch=1,
            grid=(n // blocks,),
            in_specs=[pl.BlockSpec(c.shape, lambda i, q: (0, 0, 0)) for c in cots]
            + [pl.BlockSpec((blocks, chips, rows, cols), lambda i, q: (i, 0, 0, 0))] * 2,
            out_specs=[pl.BlockSpec((tok, blocks * rows), lambda i, q: (0, i))] * 4,
        ),
        compiler_params=pltpu.CompilerParams(vmem_limit_bytes=VMEM_LIMIT),
        cost_estimate=pl.CostEstimate(
            flops=2 * tokens * n * rows * cols * 8, bytes_accessed=16 * cols * (tokens + n * rows), transcendentals=0
        ),
        name="input_grads",
    )(at, *cots, weight, other)


def copy_kernel(n_in, n_out, plan, at_ref, *refs):
    ins, outs, sems = refs[:n_in], refs[n_in : n_in + n_out], refs[n_in + n_out]
    copies = [pltpu.make_async_copy(*pair, sems.at[i]) for i, pair in enumerate(plan(at_ref, ins, outs))]
    for copy in copies:
        copy.start()
    for copy in copies:
        copy.wait()


def copy_call(plan, n_copies, ins, outs, at, name, vmem=16 * 1024 * 1024):
    any_spec = pl.BlockSpec(memory_space=pltpu.HBM)
    moved = sum(2 * math.prod(o.shape) * o.dtype.itemsize for o in outs)
    return pl.pallas_call(
        functools.partial(copy_kernel, len(ins), len(outs), plan),
        out_shape=outs,
        grid_spec=pltpu.PrefetchScalarGridSpec(
            num_scalar_prefetch=1,
            grid=(1,),
            in_specs=[any_spec] * len(ins),
            out_specs=[pl.BlockSpec(o.shape, lambda i, a, n=len(o.shape): (0,) * n) for o in outs],
            scratch_shapes=[pltpu.SemaphoreType.DMA((n_copies,))],
        ),
        compiler_params=pltpu.CompilerParams(vmem_limit_bytes=vmem),
        cost_estimate=pl.CostEstimate(flops=0, bytes_accessed=moved, transcendentals=0),
        name=name,
    )(at, *ins)


def part_of(ref, index, size):
    return ref.at[pl.ds(pl.multiple_of(index * size, size), size)]


def pack_plan(tok, at, ins, outs):
    return [
        (part_of(cot, at[s], tok), out.at[pl.ds(i * tok, tok)]) for s, out in zip((1, 2, 3), outs) for i, cot in enumerate(ins)
    ]


def unpack_plan(tok, at, ins, outs):
    cot, other, *got = ins
    pairs = [(part_of(cot, at[0], tok), outs[0].at[0]), (part_of(other, at[0], tok), outs[0].at[1])]
    return pairs + [(g.at[pl.ds(i * tok, tok)], outs[0].at[2 * s + 2 + i]) for s, g in enumerate(got) for i in (0, 1)]


def place_plan(width, at, ins, outs):
    return [(r, outs[0].at[:, pl.ds(pl.multiple_of(at[8 + i] * width, width), width)]) for i, r in enumerate(ins)]


def per_device(activations, cotangent, weight, residual, warm_factor):
    iy, iz, ix, ic = (lax.axis_index(a) for a in ("y", "z", "x", "core"))
    tok, d = activations.shape
    tok_dev, cols = cotangent.shape
    rank = warm_factor.shape[1]
    residual = residual[0]
    scale = tok_dev ** (-0.5)
    quarter = d // 4
    sub = quarter // 4

    like = lambda *shape: jax.ShapeDtypeStruct(shape, BF16)
    w_send = lax.dynamic_slice_in_dim(weight, iz * quarter + iy * sub, sub, 0)
    w_all = lax.all_gather(w_send, ("y", "x")).reshape(4, 4, sub, cols)

    cot_other = shift(cotangent, "core", 1)
    at = [((ix + s) % 4) * 2 + ic for s in range(4)] + [(ix - s) % 4 for s in range(4)]
    at = jnp.stack(at + [(iz + s) % 4 for s in (0, 1, -1, 2)]).astype(jnp.int32)
    packed = copy_call(functools.partial(pack_plan, tok), 6, [cotangent, cot_other], [like(2 * tok, cols)] * 3, at, "pack", VMEM_LIMIT)

    warm3 = jnp.concatenate(split3(warm_factor.T), 0)
    cw = fold3(mm(warm3, cotangent, 1, 1)) * scale
    cw = reduce_scatter(cw.reshape(rank, 4, 2 * tok).transpose(1, 0, 2), "x")
    left = fold3(mm(warm3, residual, 1, 1))
    act, cw, left, *packed = lax.optimization_barrier((activations, cw, left, *packed))
    got = [shift(p, "x", s) for s, p in zip((1, 2, 3), packed)]
    gathered = lax.all_gather(act, ("x", "core"), axis=0, tiled=True)
    cw = reduce_scatter(cw.reshape(rank, 2, tok).transpose(1, 0, 2), "core")

    cw3 = jnp.concatenate(split3(cw), 0)
    left = left + fold3(mm(cw3, activations, 1, 0))
    tiles = left.reshape(rank // 8, 8, d // 128, 128).transpose(0, 2, 1, 3).reshape(-1, 8, 128)
    n_tiles = tiles.shape[0]
    part = reduce_scatter(tiles.reshape(2, n_tiles // 2, 8, 128), "core")

    part = reduce_scatter(part.reshape(4, n_tiles // 8, 8, 128), "z")
    part, *got = lax.optimization_barrier((part, *got))

    (cot_own,) = copy_call(
        functools.partial(unpack_plan, tok), 8, [cotangent, cot_other] + got, [like(8, tok, cols)], at, "unpack"
    )
    part, cot_own = lax.optimization_barrier((part, cot_own))
    c_low, c_high = shift(cot_own, "z", 1), shift(cot_own, "z", -1)
    part = reduce_scatter(part.reshape(4, n_tiles // 32, 8, 128), "y")
    part = all_sum(part, "x")
    part, c_low, c_high, w_all = lax.optimization_barrier((part, c_low, c_high, w_all))
    w_other = shift(w_all, "core", 1)
    half = tok // 2
    c_far = [shift(c_low[:, :half], "z", 1), shift(c_high[:, half:], "z", -1)]
    part = all_blocks(part, ("z", "y")).reshape(-1, 8, 128)
    grads = input_call([cot_own, c_low, c_high, *c_far], w_all, w_other, at, 2)
    part, *grads = lax.optimization_barrier((part, *grads))
    back = [grads[0], shift(grads[1], "z", -1), shift(grads[2], "z", 1), shift(grads[3], "z", 2)]
    part = both_cores(part)
    left = part.reshape(rank // 8, d // 128, 8, 128).transpose(0, 2, 1, 3).reshape(rank, d)

    left3 = jnp.concatenate(split3(left), 0)
    right = fold3(mm(left3, activations, 1, 1)) * scale
    right = both_cores(right)
    pieces = [right] + [shift(right, "x", s) for s in (1, 2, 3)]
    right = [sum(jnp.where((ix - s) % 4 == k, p, 0.0) for s, p in enumerate(pieces)) for k in range(4)]
    right = jnp.concatenate([r[c] for r in right for c in (0, 1)], 1)
    right3 = jnp.concatenate(split3(right), 0)
    sums = fold3(mm(right3, cotangent, 1, 0)) + fold3(mm(left3, residual, 1, 0))
    left, right = lax.optimization_barrier((left, right))
    inverse = inverse_of_factor(left)
    sums = all_sum(sums, "y")
    sums, inverse, *back = lax.optimization_barrier((sums, inverse, *back))
    (input_grads,) = copy_call(functools.partial(place_plan, quarter), 4, back, [like(tok, d)], at, "place")
    sums = all_sum(sums, "z")
    factor = jnp.dot(inverse, sums, precision=lax.Precision.HIGHEST) * (1.0 / 16)
    sizes = [d // 12 * w for w in (1, 2, 2, 2, 2, 2, 1)] if d % 1536 == 0 else [d // 2] * 2
    new_residual = residual_call(scale, gathered, cotangent, residual, left, inverse, factor, sizes)
    return factor.T, new_residual[None], input_grads


def solution(mesh):
    fine = Mesh(mesh.devices.reshape(4, 4, 4, 2), ("y", "z", "x", "core"))
    dp, tensor = ("y", "z"), ("x", "core")
    in_specs = (
        P(dp + tensor, None),
        P(dp, tensor),
        P(None, tensor),
        P(dp, None, tensor),
        P(tensor, None),
    )
    out_specs = (P(tensor, None), P(dp, None, tensor), P(dp + tensor, None))
    return jax.shard_map(per_device, mesh=fine, in_specs=in_specs, out_specs=out_specs, check_vma=False)
```
